256 devices in a mesh: vx: 16 (over z_lo, x, core), vy: 4 (over y), scan: 4 (over z_hi).
Axes of the slice: x: 4, y: 4, z: 8 (z_hi: 4, z_lo: 2; z = z_hi * 2 + z_lo), core: 2. Of those that a mesh axis runs over, the one named last changes fastest.
Arguments:
- volume: bfloat16 [2, 512, 256, 256], P(None, 'vx', 'vy'), may hold values from -6 to 6
- tile_matrix: bfloat16 [4, 16, 8, 1024, 128], P('scan', 'vx', 'vy'), may hold values from -0.03125 to 0.03125
- tile_offset: int32 [4, 16, 8], P('scan', 'vx', 'vy'), may hold values from 0 to 384
- patch_count: int32 [4, 64], P('scan', ('vx', 'vy')), may hold values from 1 to 3, as said below
- scan_position: int32 [4, 64, 3, 2], P('scan', ('vx', 'vy')), may hold values from 0 to 256, as said below
- measured: float32 [4, 64, 3, 256, 256], P('scan', ('vx', 'vy')), may hold values from 0.2 to 5
- illumination: float32 [2, 256, 256], replicated, may hold values from -6 to 6
Outputs:
- change: float32 [2, 512, 256, 256], P(None, 'vx', 'vy', 'scan')
The draws below stay inside these ranges and needn't reach their ends.
Inputs may be any that keep to these rules, and one draw needn't show every extreme that they name: `patch_count`: an owner's slots below its count hold measured patches, the others are unused; at every angle some owner holds 3. `scan_position`: column 0 is a patch's first detector column, 0 to 256; column 1 its first row, 0 to 0.
All inputs are finite; a program needn't handle non-finite values.
Results may differ from the reference program's by a relative error of at most 0.0085.
Values may be sent and summed in bfloat16 or wider, within the bound.
A program may use at most 64 MiB of HBM per device.

```python
import math
import jax
import jax.numpy as jnp
from jax import lax

TILE = 32
TXD = 1
TYD = 2
NZ = 256
U = 512
TU = 128
PATCH_SIDE = 256
CAP = 3
ITERS = 1
ANGLES = 4
OWNERS = 64
NX = 512
NY = 256
N_VX = 16
N_VY = 4


def draw_patch_count(key, part):
    level_key, owner_key = jax.random.split(key)
    levels = jax.random.randint(level_key, (ANGLES, OWNERS), 0, 8)
    counts = jnp.where(levels == 0, CAP, jnp.where(levels == 1, CAP - 1, 1 + levels % 2))
    chosen = jax.random.randint(owner_key, (ANGLES, 1), 0, OWNERS)
    owners_row = jnp.arange(OWNERS)[None, :]
    return jnp.where(owners_row == chosen, CAP, counts).astype(jnp.int32)


def draw_scan_position(key, part):
    column_key, row_key = jax.random.split(jax.random.fold_in(key, 7))
    columns = jax.random.randint(column_key, (ANGLES, OWNERS, CAP, 1), 0, U - PATCH_SIDE + 1)
    first_rows = jax.random.randint(row_key, (ANGLES, OWNERS, CAP, 1), 0, NZ - PATCH_SIDE + 1)
    return jnp.concatenate([columns, first_rows], axis=3).astype(jnp.int32)


def touch_ends(array, stream_key, least, largest):
    index_at = [jax.random.randint(jax.random.fold_in(stream_key, axis), (), 0, length) for axis, length in enumerate(array.shape)]
    widest = array.shape.index(max(array.shape))
    neighbour = index_at[:widest] + [(index_at[widest] + 1) % array.shape[widest]] + index_at[widest + 1:]
    return array.at[tuple(index_at)].set(least).at[tuple(neighbour)].set(largest)


def steps_of(rng, extent, cuts, low, largest):
    factor_of = 1.0
    for axis_at, parts in cuts:
        heights = jax.random.uniform(jax.random.fold_in(jax.random.fold_in(rng, 6), axis_at), (parts,), jnp.float32, low / len(cuts), largest / len(cuts))
        factor_of = factor_of * jnp.repeat(jnp.exp(heights), extent[axis_at] // parts).reshape((-1,) + (1,) * (len(extent) - 1 - axis_at))
    return factor_of


def bell_draw(rng, dims, deviation, most, shards=(), kind=jnp.bfloat16):
    loudness = steps_of(rng, dims, shards, -0.22, 0.18) if shards else 1.0
    drawn = jax.random.normal(rng, dims, jnp.float32) * deviation * loudness
    return jnp.minimum(jnp.maximum(drawn, -most), most).astype(kind)


def setup_inputs(seed: int = 0) -> dict:
    splits = jax.random.split(jax.random.key(seed), 8)
    volume = bell_draw(splits[0], (2, NX, NY, NZ), 1.0, 6.0, ((1, 16), (2, 4)))
    tile_matrix = bell_draw(splits[1], (ANGLES, TXD * N_VX, TYD * N_VY, TILE * TILE, TU), (TILE * TILE * TXD * TYD * N_VX * N_VY * TU // U) ** -0.5, 0.03125, ((0, 4), (1, 16), (2, 4)))
    tile_offset = touch_ends(jax.random.randint(splits[2], (ANGLES, TXD * N_VX, TYD * N_VY), 0, U - TU + 1), jax.random.fold_in(splits[2], 1), 0, U - TU).astype(jnp.int32)
    patch_count = draw_patch_count(jax.random.fold_in(splits[7], 71), 0)
    scan_position = draw_scan_position(jax.random.fold_in(splits[7], 71), 0)
    measured = jnp.clip(jnp.exp(math.log(5.0) - 3.218876 * jax.random.uniform(splits[5], (ANGLES, OWNERS, CAP, PATCH_SIDE, PATCH_SIDE), jnp.float32) ** steps_of(splits[5], (ANGLES, OWNERS, CAP, PATCH_SIDE, PATCH_SIDE), ((0, 4), (1, 64)), -0.2, 0.2)), 0.2, 5.0)
    illumination = bell_draw(splits[6], (2, PATCH_SIDE, PATCH_SIDE), 1.0, 6.0, (), jnp.float32)
    return dict(volume=volume, tile_matrix=tile_matrix, tile_offset=tile_offset, patch_count=patch_count, scan_position=scan_position, measured=measured, illumination=illumination)


ABSORPTION = 0.2
STEP_LENGTH = 0.003

def dft_tables(length):
    counter = jnp.arange(length, dtype=jnp.int32)
    product = counter[:, None] * counter[None, :] % length
    radians = product.astype(jnp.float32) * (2.0 * math.pi / length)
    scaling = 1.0 / math.sqrt(length)
    return (jnp.cos(radians) * scaling, jnp.sin(radians) * scaling)

def matmul(left, right):
    return jnp.dot(left, right, precision=lax.Precision.HIGHEST)

def patch_misfit(window, illumination, intensity, cosine_table, sine_table):
    amplitude = jnp.exp(-ABSORPTION * window[1])
    trans_re = amplitude * jnp.cos(window[0])
    trans_im = amplitude * jnp.sin(window[0])
    exit_re = illumination[0] * trans_re - illumination[1] * trans_im
    exit_im = illumination[0] * trans_im + illumination[1] * trans_re
    half_re = matmul(cosine_table, exit_re) + matmul(sine_table, exit_im)
    half_im = matmul(cosine_table, exit_im) - matmul(sine_table, exit_re)
    far_re = matmul(half_re, cosine_table) + matmul(half_im, sine_table)
    far_im = matmul(half_im, cosine_table) - matmul(half_re, sine_table)
    residue = far_re * far_re + far_im * far_im - intensity
    return jnp.sum(residue * residue)

def place_patch(summed_total, slope, corner):
    anchor = (jnp.zeros((), jnp.int32), corner[0].astype(jnp.int32), corner[1].astype(jnp.int32))
    before = lax.dynamic_slice(summed_total, anchor, slope.shape)
    return lax.dynamic_update_slice(summed_total, before + slope, anchor)

def volume_tiles(field):
    components, width_x, width_y, depth_cells = field.shape
    blocks = field.reshape(components, width_x // TILE, TILE, width_y // TILE, TILE, depth_cells)
    blocks = blocks.transpose(1, 3, 0, 2, 4, 5)
    return blocks.reshape(-1, components, TILE * TILE, depth_cells)

def tiles_volume(blocks, width_x, width_y):
    components = blocks.shape[1]
    depth_cells = blocks.shape[3]
    shaped = blocks.reshape(width_x // TILE, width_y // TILE, components, TILE, TILE, depth_cells)
    return shaped.transpose(2, 0, 3, 1, 4, 5).reshape(components, width_x, width_y, depth_cells)

def project(current, matrices, offsets):
    blocks = volume_tiles(current)
    flat_mats = matrices.reshape(-1, TILE * TILE, TU)
    flat_offsets = offsets.reshape(-1).astype(jnp.int32)

    def add_tile(summed_total, item):
        weights, offset, block = item
        part_sum = jnp.einsum('ku,ckz->cuz', weights.astype(jnp.float32), block.astype(jnp.float32))
        anchor = (jnp.zeros((), jnp.int32), offset, jnp.zeros((), jnp.int32))
        before = lax.dynamic_slice(summed_total, anchor, part_sum.shape)
        return (lax.dynamic_update_slice(summed_total, before + part_sum, anchor), None)
    start_sum = jnp.zeros((2, U, NZ), jnp.float32)
    summed_total, ignored_value = lax.scan(add_tile, start_sum, (flat_mats, flat_offsets, blocks))
    return summed_total

def misfit_image(projected_field, counts, positions, intensity_values, illumination, cosine_table, sine_table):
    slot_ids = jnp.arange(CAP, dtype=jnp.int32)
    active_mask = (slot_ids[None, :] < counts[:, None]).reshape(-1)
    flattened_positions = positions.reshape(-1, 2).astype(jnp.int32)
    flattened_measurements = intensity_values.reshape(-1, PATCH_SIDE, PATCH_SIDE)
    slope_fn = jax.grad(patch_misfit)

    def slot_to_add(summed_total, item):
        is_live, corner, intensity = item

        def compute(running):
            anchor = (jnp.zeros((), jnp.int32), corner[0], corner[1])
            window = lax.dynamic_slice(projected_field, anchor, (2, PATCH_SIDE, PATCH_SIDE))
            slope = slope_fn(window, illumination, intensity, cosine_table, sine_table)
            return place_patch(running, slope, corner)

        def skipped(running):
            return running
        return (lax.cond(is_live, compute, skipped, summed_total), None)
    summed_total, ignored_value = lax.scan(slot_to_add, jnp.zeros_like(projected_field), (active_mask, flattened_positions, flattened_measurements))
    return summed_total

def backproject(image, matrices, offsets):
    flat_mats = matrices.reshape(-1, TILE * TILE, TU)
    flat_offsets = offsets.reshape(-1).astype(jnp.int32)

    def cut_window(offset):
        anchor = (jnp.zeros((), jnp.int32), offset, jnp.zeros((), jnp.int32))
        return lax.dynamic_slice(image, anchor, (2, TU, NZ))
    windows = jax.vmap(cut_window)(flat_offsets).astype(jnp.bfloat16)
    blocks = jnp.einsum('tku,tcuz->tckz', flat_mats.astype(jnp.float32), windows.astype(jnp.float32))
    return tiles_volume(blocks, NX, NY)

def reference(volume, tile_matrix, tile_offset, patch_count, scan_position, measured, illumination):
    cosine_table, sine_table = dft_tables(PATCH_SIDE)
    iterate = volume.astype(jnp.float32)
    current = volume
    for iteration in range(ITERS):
        slope_sum = jnp.zeros(volume.shape, jnp.float32)
        for angle_index in range(ANGLES):
            projected_field = project(current, tile_matrix[angle_index], tile_offset[angle_index])
            image = misfit_image(projected_field, patch_count[angle_index], scan_position[angle_index], measured[angle_index], illumination, cosine_table, sine_table)
            slope = backproject(image, tile_matrix[angle_index], tile_offset[angle_index])
            rounded = lax.optimization_barrier(slope.astype(jnp.bfloat16))
            slope_sum = slope_sum + rounded.astype(jnp.float32)
        iterate = iterate - STEP_LENGTH * slope_sum
        current = iterate.astype(jnp.bfloat16)
    return iterate - volume.astype(jnp.float32)
```

```python
import functools
import math

import jax
import jax.numpy as jnp
import numpy as np
from jax import lax
from jax.experimental import pallas as pl
from jax.experimental.pallas import tpu as pltpu
from jax.sharding import PartitionSpec as P

MESH = pl.DeviceIdType.MESH
BF = jnp.bfloat16
F32 = jnp.float32

ABSORPTION = 0.2
STEP_LENGTH = 0.003
SIDE = 256
CAP = 3

PROJ_WIRE = BF
PROJ_FULL = F32
IMAGE_WIRE = BF

CORE_P, CORE_I = 0, 1
MATS = 2
OFFS = 8
RS_P, RS_I = 11, 23
Z_P = 35
Z_I = 36
AG_P, AG_I = 44, 56
CORE_GP, CORE_GI = 68, 69
N_SEMS = 70


def tables():
    n = np.arange(SIDE)
    angle = 2.0 * math.pi * (n[:, None] * n[None, :] % SIDE) / SIDE
    cosine = np.cos(angle) / math.sqrt(SIDE)
    sine = np.sin(angle) / math.sqrt(SIDE)
    first = np.block([[cosine, sine], [-sine, cosine]])
    high = first.astype(BF)
    low = (first - high.astype(np.float64)).astype(BF)
    return np.stack([high, low, high.T, low.T])


def sin_cos(value):
    turns = jnp.floor(value * (2.0 / math.pi) + 0.5)
    rest = value - turns * 1.5703125
    rest = rest - turns * 4.837512969970703125e-4
    rest = rest - turns * 7.54978995489188216e-8
    square = rest * rest
    sine = ((-1.9515295891e-4 * square + 8.3321608736e-3) * square - 1.6666654611e-1) * square * rest + rest
    cosine = ((2.443315711809948e-5 * square - 1.388731625493765e-3) * square + 4.166664568298827e-2) * square * square
    cosine = cosine - 0.5 * square + 1.0
    quadrant = turns.astype(jnp.int32)
    odd = (quadrant & 1) == 1
    flip_sine = (quadrant & 2) == 2
    flip_cosine = ((quadrant + 1) & 2) == 2
    s = jnp.where(odd, cosine, sine)
    c = jnp.where(odd, sine, cosine)
    return jnp.where(flip_sine, -s, s), jnp.where(flip_cosine, -c, c)


def dot(left, right):
    return jnp.dot(left, right, preferred_element_type=F32)


def halves(value):
    high = value.astype(BF)
    return high, (value - high.astype(F32)).astype(BF)


def kernel(
    offset_ref,
    count_ref,
    position_ref,
    volume_hbm,
    matrix_hbm,
    measured_hbm,
    probe_hbm,
    table_hbm,
    out_hbm,
    volume,
    matrix,
    measured,
    probe,
    table,
    matrices,
    offsets,
    tile_pad,
    grad_pad,
    s1,
    r1,
    acc1,
    s2,
    r2,
    acc2,
    s3,
    r3,
    sz,
    rz,
    full,
    window,
    t1,
    q1,
    t2,
    q2,
    t3,
    q3,
    zs,
    zr,
    slabs,
    out,
    load_sem,
    ssem,
    rsem,
):
    vx, y, s = lax.axis_index("vx"), lax.axis_index("vy"), lax.axis_index("scan")
    zl, x, c = vx // 8, (vx // 2) % 4, vx % 2

    def at(zl=zl, x=x, c=c, y=y, s=s):
        return (zl * 8 + x * 2 + c, y, s)

    def turn(index, d):
        return lax.rem(index + d, 4)

    def remote(number, src, dst, device):
        return pltpu.make_async_remote_copy(
            src_ref=src,
            dst_ref=dst,
            send_sem=ssem.at[number],
            recv_sem=rsem.at[number],
            device_id=device,
            device_id_type=MESH,
        )

    loads = [
        pltpu.make_async_copy(src, dst, load_sem.at[i])
        for i, (src, dst) in enumerate(
            [
                (volume_hbm, volume),
                (matrix_hbm, matrix),
                (measured_hbm, measured),
                (probe_hbm, probe),
                (table_hbm, table),
            ]
        )
    ]
    for load in loads:
        load.start()

    across = at(c=1 - c)
    partners = [across]
    partners += [at(x=turn(x, d)) for d in (1, 2, 3)]
    partners += [at(y=turn(y, d)) for d in (1, 2, 3)]
    column = [(dz, d) for dz in (0, 1) for d in range(4) if dz or d]
    partners += [at(zl=lax.rem(zl + dz, 2), s=turn(s, d)) for dz, d in column]
    barrier = pltpu.get_barrier_semaphore()
    for partner in partners:
        pl.semaphore_signal(barrier, inc=1, device_id=partner, device_id_type=MESH)

    for t in range(2):
        tile_pad[t, :, 0:384, :] = jnp.zeros((4, 384, 128), F32)
        tile_pad[t, :, 512:896, :] = jnp.zeros((4, 384, 128), F32)
    for k in range(CAP):
        grad_pad[k, :, 0:256, :] = jnp.zeros((4, 256, 128), F32)
        grad_pad[k, :, 512:768, :] = jnp.zeros((4, 256, 128), F32)
    for t in range(2):
        offsets[0, t] = jnp.full((8, 128), offset_ref[0, 0, t], jnp.int32)

    pl.semaphore_wait(barrier, len(partners))

    sent = []
    first_round = []
    for i, d in enumerate((1, 3)):
        for t in range(2):
            copy = remote(MATS + 2 * i + t, matrix_hbm.at[t], matrices.at[4 - d - 1, t], at(s=turn(s, d)))
            first_round.append(copy)
    for d in (1, 2, 3):
        copy = remote(OFFS + d - 1, offsets.at[0], offsets.at[4 - d], at(s=turn(s, d)))
        copy.start()
        sent.append(copy)

    loads[0].wait()
    loads[1].wait()
    for t in range(2):
        for part in range(2):
            block = volume[part, :, 32 * t : 32 * t + 32, :].reshape(1024, 256)
            shadow = lax.dot_general(
                matrix[t], block, (((0,), (0,)), ((), ())), preferred_element_type=F32
            )
            for j in range(2):
                tile_pad[t, 2 * part + j, 384:512, :] = shadow[:, 128 * j : 128 * j + 128]

    def placed(padded, starts, h):
        blocks = []
        for j in range(2):
            terms = [padded[i, 2 * h + j, pl.ds(start, 256), :] for i, start in enumerate(starts)]
            blocks.append(functools.reduce(jnp.add, terms))
        return jnp.concatenate(blocks, axis=1).reshape(4, 4, 16, 256)

    def placed_tiles(h, first):
        return placed(tile_pad, [384 - offset_ref[0, 0, t] + first for t in range(2)], h)

    def reduced(source, s1, r1, core_number, s2, r2, s3, r3, numbers, wire):
        for h in range(2):
            s1[h] = source(h, (1 - c) * 256).astype(wire)
        copy = remote(core_number, s1, r1, across)
        copy.start()
        sent.append(copy)
        for h in range(2):
            acc1[h] = source(h, c * 256)
        copy.wait_recv()
        copies = [[], []]
        for h in range(2):
            value = acc1[h] + r1[h].astype(F32)
            acc1[h] = value
            s2[h] = value.astype(wire)
            for d in (1, 2, 3):
                if h == 0:
                    to = turn(x, d)
                    copy = remote(numbers + d - 1, s2.at[0, to], r2.at[0, d - 1], at(x=to))
                else:
                    to = turn(y, d)
                    copy = remote(numbers + 3 + d - 1, s2.at[1, :, to], r2.at[1, d - 1], at(y=to))
                copy.start()
                sent.append(copy)
                copies[h].append(copy)
        later = [[], []]
        for h in range(2):
            value = acc1[0, x] if h == 0 else acc1[1, :, y]
            for d in (1, 2, 3):
                copies[h][d - 1].wait_recv()
            for d in (1, 2, 3):
                value = value + r2[h, d - 1].astype(F32)
            acc2[h] = value
            s3[h] = value.astype(wire)
            for d in (1, 2, 3):
                to = turn(y if h == 0 else x, d)
                device = at(y=to) if h == 0 else at(x=to)
                copy = remote(numbers + 6 + 3 * h + d - 1, s3.at[h, to], r3.at[h, d - 1], device)
                copy.start()
                sent.append(copy)
                later[h].append(copy)
        result = []
        for h in range(2):
            value = acc2[h, y if h == 0 else x]
            for d in (1, 2, 3):
                later[h][d - 1].wait_recv()
            for d in (1, 2, 3):
                value = value + r3[h, d - 1].astype(F32)
            result.append(value)
        return result

    def gathered(whole, n, numbers, core_number):
        copies = [[], []]
        for h in range(2):
            for d in (1, 2, 3):
                block = whole.at[pl.ds(n * h, n), c, x, y]
                device = at(y=turn(y, d)) if h == 0 else at(x=turn(x, d))
                copy = remote(numbers + 3 * h + d - 1, block, block, device)
                copy.start()
                sent.append(copy)
                copies[h].append(copy)
        later = []
        for h in range(2):
            for copy in copies[h]:
                copy.wait_recv()
            for d in (1, 2, 3):
                block = whole.at[pl.ds(0, n), c, x] if h == 0 else whole.at[pl.ds(n, n), c, :, y]
                device = at(x=turn(x, d)) if h == 0 else at(y=turn(y, d))
                copy = remote(numbers + 6 + 3 * h + d - 1, block, block, device)
                copy.start()
                sent.append(copy)
                later.append(copy)
        for copy in later:
            copy.wait_recv()
        block = whole.at[:, c]
        copy = remote(core_number, block, block, across)
        copy.start()
        sent.append(copy)
        copy.wait_recv()

    block = reduced(placed_tiles, s1, r1, CORE_P, s2, r2, s3, r3, RS_P, PROJ_WIRE)
    for h in range(2):
        sz[h] = block[h].astype(sz.dtype)
    copy = remote(Z_P, sz, rz, at(zl=1 - zl))
    copy.start()
    sent.append(copy)
    copy.wait_recv()
    for h in range(2):
        full[h, c, x, y] = (block[h] + rz[h].astype(F32)).astype(full.dtype)
    for copy in first_round:
        copy.start()
    gathered(full, 1, AG_P, CORE_GP)
    for h in range(2):
        projection = full[h].reshape(512, 256).astype(F32)
        for j in range(2):
            window[h, j] = projection[:, 128 * j : 128 * j + 128]

    for load in loads[2:]:
        load.wait()
    lane = lax.broadcasted_iota(jnp.int32, (256, 128), 1)
    for k in range(CAP):
        rows = pl.ds(position_ref[0, 0, k, 0], 256)
        phase, loss = (
            jnp.concatenate([window[part, j, rows, :] for j in range(2)], axis=1) for part in range(2)
        )
        sine, cosine = sin_cos(phase)
        amplitude = jnp.exp(-ABSORPTION * loss)
        cosine, sine = amplitude * cosine, amplitude * sine
        exit_re = probe[0] * cosine - probe[1] * sine
        exit_im = probe[0] * sine + probe[1] * cosine

        def left(which, value):
            high, low = halves(value)
            return dot(table[which], high) + dot(table[which], low) + dot(table[which + 1], high)

        def right(value, which):
            high, low = halves(value)
            return dot(high, table[which]) + dot(low, table[which]) + dot(high, table[which + 1])

        half = left(0, jnp.concatenate([exit_re, exit_im], axis=0))
        far = right(jnp.concatenate([half[:256], half[256:]], axis=1), 2)
        far_re, far_im = far[:, :256], far[:, 256:]
        residue = 4.0 * (far_re * far_re + far_im * far_im - measured[k])
        back = left(2, jnp.concatenate([residue * far_re, residue * far_im], axis=0))
        grad = right(jnp.concatenate([back[:256], back[256:]], axis=1), 0)
        grad_re, grad_im = grad[:, :256], grad[:, 256:]
        live = k < count_ref[0, 0]
        by_phase = jnp.where(live, grad_im * exit_re - grad_re * exit_im, 0.0)
        by_loss = jnp.where(live, -ABSORPTION * (grad_re * exit_re + grad_im * exit_im), 0.0)
        for h in range(2):
            a, b = by_phase[:, 128 * h : 128 * h + 128], by_loss[:, 128 * h : 128 * h + 128]
            even = jnp.where(lane < 64, a, pltpu.roll(b, 64, 1))
            odd = jnp.where(lane < 64, pltpu.roll(a, 64, 1), b)
            grad_pad[k, 2 * h, 256:512, :] = even
            grad_pad[k, 2 * h + 1, 256:512, :] = odd

    def placed_patches(h, first):
        return placed(grad_pad, [256 - position_ref[0, 0, k, 0] + first for k in range(CAP)], h)

    for copy in first_round:
        copy.wait_recv()
    second_round = [
        remote(MATS + 4, matrices.at[2, 0], matrices.at[1, 0], at(s=turn(s, 1))),
        remote(MATS + 5, matrices.at[0, 1], matrices.at[1, 1], at(s=turn(s, 3))),
    ]
    for copy in second_round:
        copy.start()

    block = reduced(placed_patches, t1, q1, CORE_I, t2, q2, t3, q3, RS_I, IMAGE_WIRE)
    for h in range(2):
        for j in range(2):
            zs[2 * h + j] = block[h][:, 128 * j : 128 * j + 128].astype(zs.dtype)
    zr[0, 0] = zs[s]
    copies = []
    for i, (dz, d) in enumerate(column):
        to = turn(s, d)
        copy = remote(Z_I + i, zs.at[to], zr.at[dz, (4 - d) % 4], at(zl=lax.rem(zl + dz, 2), s=to))
        copy.start()
        copies.append(copy)
        sent.append(copy)
    for copy in copies:
        copy.wait_recv()
    for k in range(4):
        slabs[k, c, x, y] = (zr[0, k].astype(F32) + zr[1, k].astype(F32)).astype(BF)
    gathered(slabs, 2, AG_I, CORE_GI)

    for copy in sent[:3]:
        copy.wait_recv()
    columns = lax.broadcasted_iota(jnp.int32, (128, 512), 1) - lax.broadcasted_iota(jnp.int32, (128, 512), 0)
    windows = []
    for t in range(2):
        pieces = []
        for k in range(4):
            first = jnp.broadcast_to(offsets[k, t][0:1, 0:1], (128, 512))
            chosen = jnp.where(columns == first, 1.0, 0.0).astype(BF)
            pieces.append(dot(chosen, slabs[k].reshape(512, 128)).astype(BF))
        windows.append(jnp.concatenate(pieces, axis=0))
    for copy in second_round:
        copy.wait_recv()
    stores = []
    for t in range(2):
        weights = jnp.concatenate([matrix[t], matrices[0, t], matrices[1, t], matrices[2, t]], axis=1)
        slope = (-STEP_LENGTH * dot(weights, windows[t])).reshape(32, 32, 128)
        for part in range(2):
            out[part, :, 32 * t : 32 * t + 32, :] = slope[:, :, 64 * part : 64 * part + 64]
        cut = pl.ds(32 * t, 32)
        store = pltpu.make_async_copy(out.at[:, :, cut, :], out_hbm.at[:, :, cut, :], load_sem.at[5 + t])
        store.start()
        stores.append(store)
    for store in stores:
        store.wait()
    for copy in sent + first_round + second_round:
        copy.wait_send()


def per_device(volume, tile_matrix, tile_offset, patch_count, scan_position, measured, illumination):
    any_space = pl.BlockSpec(memory_space=pl.ANY)
    smem = pl.BlockSpec(memory_space=pltpu.SMEM)
    wire = lambda kind: [
        pltpu.VMEM((2, 4, 4, 16, 256), kind),
        pltpu.VMEM((2, 4, 4, 16, 256), kind),
    ]
    return pl.pallas_call(
        kernel,
        out_shape=jax.ShapeDtypeStruct((2, 32, 64, 64), F32),
        in_specs=[smem] * 3 + [any_space] * 5,
        out_specs=any_space,
        scratch_shapes=[
            pltpu.VMEM((2, 32, 64, 256), BF),
            pltpu.VMEM((2, 1024, 128), BF),
            pltpu.VMEM((3, 256, 256), F32),
            pltpu.VMEM((2, 256, 256), F32),
            pltpu.VMEM((4, 512, 512), BF),
            pltpu.VMEM((3, 2, 1024, 128), BF),
            pltpu.VMEM((4, 2, 8, 128), jnp.int32),
            pltpu.VMEM((2, 4, 896, 128), F32),
            pltpu.VMEM((3, 4, 768, 128), F32),
            *wire(PROJ_WIRE),
            pltpu.VMEM((2, 4, 4, 16, 256), F32),
            pltpu.VMEM((2, 4, 4, 16, 256), PROJ_WIRE),
            pltpu.VMEM((2, 3, 4, 16, 256), PROJ_WIRE),
            pltpu.VMEM((2, 4, 16, 256), F32),
            pltpu.VMEM((2, 4, 16, 256), PROJ_WIRE),
            pltpu.VMEM((2, 3, 16, 256), PROJ_WIRE),
            pltpu.VMEM((2, 16, 256), F32),
            pltpu.VMEM((2, 16, 256), F32),
            pltpu.VMEM((2, 2, 4, 4, 16, 256), PROJ_FULL),
            pltpu.VMEM((2, 2, 512, 128), F32),
            *wire(IMAGE_WIRE),
            pltpu.VMEM((2, 4, 4, 16, 256), IMAGE_WIRE),
            pltpu.VMEM((2, 3, 4, 16, 256), IMAGE_WIRE),
            pltpu.VMEM((2, 4, 16, 256), IMAGE_WIRE),
            pltpu.VMEM((2, 3, 16, 256), IMAGE_WIRE),
            pltpu.VMEM((4, 16, 128), F32),
            pltpu.VMEM((2, 4, 16, 128), F32),
            pltpu.VMEM((4, 2, 4, 4, 16, 128), BF),
            pltpu.VMEM((2, 32, 64, 64), F32),
            pltpu.SemaphoreType.DMA((7,)),
            pltpu.SemaphoreType.DMA((N_SEMS,)),
            pltpu.SemaphoreType.DMA((N_SEMS,)),
        ],
        compiler_params=pltpu.CompilerParams(
            collective_id=0, has_side_effects=True, vmem_limit_bytes=60 * 2**20
        ),
    )(
        tile_offset,
        patch_count,
        scan_position,
        volume,
        tile_matrix.reshape(2, 1024, 128),
        measured.reshape(3, 256, 256),
        illumination,
        jnp.asarray(tables()),
    )


def solution(mesh):
    in_specs = (
        P(None, "vx", "vy", None),
        P("scan", "vx", "vy", None, None),
        P("scan", "vx", "vy"),
        P("scan", ("vx", "vy")),
        P("scan", ("vx", "vy"), None, None),
        P("scan", ("vx", "vy"), None, None, None),
        P(),
    )
    out_specs = P(None, "vx", "vy", "scan")
    return jax.shard_map(
        per_device, mesh=mesh, in_specs=in_specs, out_specs=out_specs, check_vma=False
    )
```

```python
import functools
import math

import jax
import jax.numpy as jnp
import numpy as np
from jax import lax
from jax.experimental import pallas as pl
from jax.experimental.pallas import tpu as pltpu
from jax.sharding import PartitionSpec as P

MESH = pl.DeviceIdType.MESH
BF = jnp.bfloat16
F32 = jnp.float32

ABSORPTION = 0.2
STEP_LENGTH = 0.003
SIDE = 256
CAP = 3

CORE_P, CORE_I, Z_P, CORE_GP, CORE_GI = range(5)
MATS = 5
OFFS = 11
RS_P, RS_I, AG_P, AG_I = 14, 29, 44, 59
Z_I = 74
N_SEMS = 81

PLANE = sorted(
    ((dx, dy) for dx in range(4) for dy in range(4) if dx or dy),
    key=lambda step: -sum(min(d, 4 - d) for d in step),
)
COLUMN = [(dz, d) for d in (2, 1, 3, 0) for dz in (1, 0) if dz or d]


def tables():
    n = np.arange(SIDE)
    angle = 2.0 * math.pi * (n[:, None] * n[None, :] % SIDE) / SIDE
    cosine = np.cos(angle) / math.sqrt(SIDE)
    sine = np.sin(angle) / math.sqrt(SIDE)
    first = np.block([[cosine, sine], [-sine, cosine]])
    return np.stack([first, first.T]).astype(BF)


def sin_cos(value):
    turns = jnp.floor(value * (2.0 / math.pi) + 0.5)
    rest = value - turns * 1.5703125
    rest = rest - turns * 4.837512969970703125e-4
    rest = rest - turns * 7.54978995489188216e-8
    square = rest * rest
    sine = ((-1.9515295891e-4 * square + 8.3321608736e-3) * square - 1.6666654611e-1) * square * rest + rest
    cosine = ((2.443315711809948e-5 * square - 1.388731625493765e-3) * square + 4.166664568298827e-2) * square * square
    cosine = cosine - 0.5 * square + 1.0
    quadrant = turns.astype(jnp.int32)
    odd = (quadrant & 1) == 1
    flip_sine = (quadrant & 2) == 2
    flip_cosine = ((quadrant + 1) & 2) == 2
    s = jnp.where(odd, cosine, sine)
    c = jnp.where(odd, sine, cosine)
    return jnp.where(flip_sine, -s, s), jnp.where(flip_cosine, -c, c)


def dot(left, right):
    return jnp.dot(left, right, preferred_element_type=F32)


def kernel(
    offset_ref,
    count_ref,
    position_ref,
    volume_hbm,
    matrix_hbm,
    measured_hbm,
    probe_hbm,
    table_hbm,
    windows_out,
    matrices,
    volume,
    matrix,
    measured,
    probe,
    table,
    offsets,
    tile_pad,
    grad_pad,
    s1,
    r1,
    acc1,
    s2,
    r2,
    sz,
    rz,
    full,
    window,
    t1,
    q1,
    acc2,
    t2,
    q2,
    zs,
    zr,
    slabs,
    load_sem,
    ssem,
    rsem,
):
    vx, y, s = lax.axis_index("vx"), lax.axis_index("vy"), lax.axis_index("scan")
    zl, x, c = vx // 8, (vx // 2) % 4, vx % 2

    def at(zl=zl, x=x, c=c, y=y, s=s):
        return (zl * 8 + x * 2 + c, y, s)

    def turn(index, d):
        return lax.rem(index + d, 4)

    def remote(number, src, dst, device):
        return pltpu.make_async_remote_copy(
            src_ref=src,
            dst_ref=dst,
            send_sem=ssem.at[number],
            recv_sem=rsem.at[number],
            device_id=device,
            device_id_type=MESH,
        )

    loads = [
        pltpu.make_async_copy(src, dst, load_sem.at[i])
        for i, (src, dst) in enumerate(
            [
                (volume_hbm, volume),
                (matrix_hbm, matrix),
                (measured_hbm, measured),
                (probe_hbm, probe),
                (table_hbm, table),
            ]
        )
    ]
    for load in loads:
        load.start()

    across = at(c=1 - c)
    plane = [at(x=turn(x, dx), y=turn(y, dy)) for dx, dy in PLANE]
    column = [at(zl=lax.rem(zl + dz, 2), s=turn(s, d)) for dz, d in COLUMN]
    barrier = pltpu.get_barrier_semaphore()
    for partner in [*column, *plane, across]:
        pl.semaphore_signal(barrier, inc=1, device_id=partner, device_id_type=MESH)

    for t in range(2):
        tile_pad[t, :, 0:384, :] = jnp.zeros((4, 384, 128), F32)
        tile_pad[t, :, 512:896, :] = jnp.zeros((4, 384, 128), F32)
    for k in range(CAP):
        grad_pad[k, :, 0:256, :] = jnp.zeros((4, 256, 128), F32)
        grad_pad[k, :, 512:768, :] = jnp.zeros((4, 256, 128), F32)
    for t in range(2):
        offsets[0, t] = jnp.full((8, 128), offset_ref[0, 0, t], jnp.int32)

    loads[0].wait()
    loads[1].wait()
    for t in range(2):
        for part in range(2):
            block = volume[part, :, 32 * t : 32 * t + 32, :].reshape(1024, 256)
            shadow = lax.dot_general(
                matrix[t], block, (((0,), (0,)), ((), ())), preferred_element_type=F32
            )
            for j in range(2):
                tile_pad[t, 2 * part + j, 384:512, :] = shadow[:, 128 * j : 128 * j + 128]

    def placed(padded, starts, h):
        blocks = []
        for j in range(2):
            terms = [padded[i, 2 * h + j, pl.ds(start, 256), :] for i, start in enumerate(starts)]
            blocks.append(functools.reduce(jnp.add, terms))
        return jnp.concatenate(blocks, axis=1).reshape(4, 4, 16, 256)

    def placed_tiles(h, first):
        return placed(tile_pad, [384 - offset_ref[0, 0, t] + first for t in range(2)], h)

    def reduced(source, s1, r1, core_number, acc, s2, r2, numbers):
        copy = remote(core_number, s1, r1, across)
        copy.start()
        sent.append(copy)
        for h in range(2):
            acc[:, :, h] = source(h, c * 256)
        copy.wait_recv()
        value = acc[...] + r1[...].astype(F32)
        acc[...] = value
        s2[...] = value.astype(BF)
        copies = []
        for i, (dx, dy) in enumerate(PLANE):
            copy = remote(numbers + i, s2.at[turn(x, dx), turn(y, dy)], r2.at[i], plane[i])
            copy.start()
            copies.append(copy)
        sent.extend(copies)
        value = acc[x, y]
        for copy in copies:
            copy.wait_recv()
        for i in range(len(PLANE)):
            value = value + r2[i].astype(F32)
        return value

    def gathered(whole, numbers, core_number):
        copies = []
        block = whole.at[c, x, y]
        for i in range(len(PLANE)):
            copy = remote(numbers + i, block, block, plane[i])
            copy.start()
            copies.append(copy)
        sent.extend(copies)
        for copy in copies:
            copy.wait_recv()
        block = whole.at[c]
        copy = remote(core_number, block, block, across)
        copy.start()
        sent.append(copy)
        copy.wait_recv()

    for h in range(2):
        s1[:, :, h] = placed_tiles(h, (1 - c) * 256).astype(BF)

    pl.semaphore_wait(barrier, 1 + len(PLANE) + len(COLUMN))
    sent = []
    first_round = []
    for i, d in enumerate((1, 3)):
        for t in range(2):
            copy = remote(MATS + 2 * i + t, matrix_hbm.at[t], matrices.at[3 - d, t], at(s=turn(s, d)))
            first_round.append(copy)
    early = []
    for d in (1, 2, 3):
        copy = remote(OFFS + d - 1, offsets.at[0], offsets.at[4 - d], at(s=turn(s, d)))
        early.append(copy)

    for copy in early:
        copy.start()
    for copy in (first_round[0], first_round[3]):
        copy.start()
    block = reduced(placed_tiles, s1, r1, CORE_P, acc1, s2, r2, RS_P)
    sz[...] = block
    copy = remote(Z_P, sz, rz, at(zl=1 - zl))
    copy.start()
    sent.append(copy)
    copy.wait_recv()
    for copy in (first_round[0], first_round[3]):
        copy.wait_recv()
    second_round = [
        remote(MATS + 4, matrices.at[2, 0], matrices.at[1, 0], at(s=turn(s, 1))),
        remote(MATS + 5, matrices.at[0, 1], matrices.at[1, 1], at(s=turn(s, 3))),
    ]
    for copy in second_round:
        copy.start()
    for copy in first_round[1:3]:
        copy.start()
    full[c, x, y] = (block + rz[...]).astype(BF)
    gathered(full, AG_P, CORE_GP)
    for h in range(2):
        projection = full[:, :, :, h].reshape(512, 256).astype(F32)
        for j in range(2):
            window[h, j] = projection[:, 128 * j : 128 * j + 128]

    for load in loads[2:]:
        load.wait()
    lane = lax.broadcasted_iota(jnp.int32, (256, 128), 1)
    for k in range(CAP):
        rows = pl.ds(position_ref[0, 0, 0, k], 256)
        phase, loss = (
            jnp.concatenate([window[part, j, rows, :] for j in range(2)], axis=1) for part in range(2)
        )
        sine, cosine = sin_cos(phase)
        amplitude = jnp.exp(-ABSORPTION * loss)
        cosine, sine = amplitude * cosine, amplitude * sine
        exit_re = probe[0] * cosine - probe[1] * sine
        exit_im = probe[0] * sine + probe[1] * cosine

        half = dot(table[0], jnp.concatenate([exit_re, exit_im], axis=0).astype(BF)).astype(BF)
        far = dot(jnp.concatenate([half[:256], half[256:]], axis=1), table[1])
        far_re, far_im = far[:, :256], far[:, 256:]
        residue = 4.0 * (far_re * far_re + far_im * far_im - measured[k])
        residue_far = jnp.concatenate([residue * far_re, residue * far_im], axis=0).astype(BF)
        back = dot(table[1], residue_far).astype(BF)
        grad = dot(jnp.concatenate([back[:256], back[256:]], axis=1), table[0])
        grad_re, grad_im = grad[:, :256], grad[:, 256:]
        live = k < count_ref[0, 0]
        by_phase = jnp.where(live, grad_im * exit_re - grad_re * exit_im, 0.0)
        by_loss = jnp.where(live, -ABSORPTION * (grad_re * exit_re + grad_im * exit_im), 0.0)
        for h in range(2):
            a, b = by_phase[:, 128 * h : 128 * h + 128], by_loss[:, 128 * h : 128 * h + 128]
            even = jnp.where(lane < 64, a, pltpu.roll(b, 64, 1))
            odd = jnp.where(lane < 64, pltpu.roll(a, 64, 1), b)
            grad_pad[k, 2 * h, 256:512, :] = even
            grad_pad[k, 2 * h + 1, 256:512, :] = odd

    def placed_patches(h, first):
        return placed(grad_pad, [256 - position_ref[0, 0, 0, k] + first for k in range(CAP)], h)

    for h in range(2):
        t1[:, :, h] = placed_patches(h, (1 - c) * 256).astype(BF)
    block = reduced(placed_patches, t1, q1, CORE_I, acc2, t2, q2, RS_I)
    for k in range(4):
        zs[k] = block[k // 2, :, 128 * (k % 2) : 128 * (k % 2) + 128]
    zr[0, 0] = zs[s]
    copies = []
    for i, (dz, d) in enumerate(COLUMN):
        copy = remote(Z_I + i, zs.at[turn(s, d)], zr.at[dz, (4 - d) % 4], column[i])
        copy.start()
        copies.append(copy)
    sent.extend(copies)
    for copy in copies:
        copy.wait_recv()
    slabs[c, x, y] = (zr[0] + zr[1]).astype(BF)
    gathered(slabs, AG_I, CORE_GI)

    for copy in early:
        copy.wait_recv()
    columns = lax.broadcasted_iota(jnp.int32, (128, 512), 1) - lax.broadcasted_iota(jnp.int32, (128, 512), 0)
    for k in range(4):
        slab = slabs[:, :, :, k].reshape(512, 128)
        for t in range(2):
            first = jnp.broadcast_to(offsets[k, t][0:1, 0:1], (128, 512))
            chosen = jnp.where(columns == first, 1.0, 0.0).astype(BF)
            windows_out[t, 128 * k : 128 * k + 128, :] = dot(chosen, slab).astype(BF)
    for copy in first_round[1:3] + second_round:
        copy.wait_recv()
    for copy in sent + early + first_round + second_round:
        copy.wait_send()


def back_kernel(windows, own_hbm, matrices_hbm, out_hbm, weights, out, load_sem, store_sem):
    loads = []
    for t in range(2):
        for k in range(4):
            source = own_hbm.at[t] if k == 0 else matrices_hbm.at[k - 1, t]
            load = pltpu.make_async_copy(source, weights.at[t, k], load_sem.at[t, k])
            load.start()
            loads.append(load)
    stores = []
    for t in range(2):
        for k in range(4):
            loads[4 * t + k].wait()
        side = jnp.concatenate([weights[t, k] for k in range(4)], axis=1)
        slope = (-STEP_LENGTH * dot(side, windows[t])).reshape(32, 32, 128)
        for part in range(2):
            out[part, :, 32 * t : 32 * t + 32, :] = slope[:, :, 64 * part : 64 * part + 64]
        cut = pl.ds(32 * t, 32)
        store = pltpu.make_async_copy(out.at[:, :, cut, :], out_hbm.at[:, :, cut, :], store_sem.at[t])
        store.start()
        stores.append(store)
    for store in stores:
        store.wait()


def per_device(volume, tile_matrix, tile_offset, patch_count, scan_position, measured, illumination):
    any_space = pl.BlockSpec(memory_space=pl.ANY)
    smem = pl.BlockSpec(memory_space=pltpu.SMEM)
    block = (4, 4, 2, 16, 256)
    tile_matrix = tile_matrix.reshape(2, 1024, 128)
    windows, matrices = pl.pallas_call(
        kernel,
        out_shape=(
            jax.ShapeDtypeStruct((2, 512, 128), BF),
            jax.ShapeDtypeStruct((3, 2, 1024, 128), BF),
        ),
        in_specs=[smem] * 3 + [any_space] * 5,
        out_specs=(pl.BlockSpec(memory_space=pltpu.VMEM), any_space),
        scratch_shapes=[
            pltpu.VMEM((2, 32, 64, 256), BF),
            pltpu.VMEM((2, 1024, 128), BF),
            pltpu.VMEM((3, 256, 256), F32),
            pltpu.VMEM((2, 256, 256), F32),
            pltpu.VMEM((2, 512, 512), BF),
            pltpu.VMEM((4, 2, 8, 128), jnp.int32),
            pltpu.VMEM((2, 4, 896, 128), F32),
            pltpu.VMEM((3, 4, 768, 128), F32),
            pltpu.VMEM(block, BF),
            pltpu.VMEM(block, BF),
            pltpu.VMEM(block, F32),
            pltpu.VMEM(block, BF),
            pltpu.VMEM((15, 2, 16, 256), BF),
            pltpu.VMEM((2, 16, 256), F32),
            pltpu.VMEM((2, 16, 256), F32),
            pltpu.VMEM((2, *block), BF),
            pltpu.VMEM((2, 2, 512, 128), F32),
            pltpu.VMEM(block, BF),
            pltpu.VMEM(block, BF),
            pltpu.VMEM(block, F32),
            pltpu.VMEM(block, BF),
            pltpu.VMEM((15, 2, 16, 256), BF),
            pltpu.VMEM((4, 16, 128), F32),
            pltpu.VMEM((2, 4, 16, 128), F32),
            pltpu.VMEM((2, 4, 4, 4, 16, 128), BF),
            pltpu.SemaphoreType.DMA((5,)),
            pltpu.SemaphoreType.DMA((N_SEMS,)),
            pltpu.SemaphoreType.DMA((N_SEMS,)),
        ],
        compiler_params=pltpu.CompilerParams(
            collective_id=0, has_side_effects=True, vmem_limit_bytes=60 * 2**20
        ),
    )(
        tile_offset,
        patch_count,
        jnp.swapaxes(scan_position, 2, 3),
        volume,
        tile_matrix,
        measured.reshape(3, 256, 256),
        illumination,
        jnp.asarray(tables()),
    )
    return pl.pallas_call(
        back_kernel,
        out_shape=jax.ShapeDtypeStruct((2, 32, 64, 64), F32),
        in_specs=[pl.BlockSpec(memory_space=pltpu.VMEM), any_space, any_space],
        out_specs=any_space,
        scratch_shapes=[
            pltpu.VMEM((2, 4, 1024, 128), BF),
            pltpu.VMEM((2, 32, 64, 64), F32),
            pltpu.SemaphoreType.DMA((2, 4)),
            pltpu.SemaphoreType.DMA((2,)),
        ],
        compiler_params=pltpu.CompilerParams(vmem_limit_bytes=60 * 2**20),
    )(windows, tile_matrix, matrices)


def solution(mesh):
    in_specs = (
        P(None, "vx", "vy", None),
        P("scan", "vx", "vy", None, None),
        P("scan", "vx", "vy"),
        P("scan", ("vx", "vy")),
        P("scan", ("vx", "vy"), None, None),
        P("scan", ("vx", "vy"), None, None, None),
        P(),
    )
    out_specs = P(None, "vx", "vy", "scan")
    return jax.shard_map(
        per_device, mesh=mesh, in_specs=in_specs, out_specs=out_specs, check_vma=False
    )
```

```python
import functools
import math

import jax
import jax.numpy as jnp
import numpy as np
from jax import lax
from jax.experimental import pallas as pl
from jax.experimental.pallas import tpu as pltpu
from jax.sharding import PartitionSpec as P

MESH = pl.DeviceIdType.MESH
BF = jnp.bfloat16
F32 = jnp.float32

ABSORPTION = 0.2
STEP_LENGTH = 0.003
SIDE = 256
CAP = 3

CORE_P, CORE_I, Z_P, CORE_GP, CORE_GI = range(5)
OFFS = 5
RS_P, RS_I, AG_P, AG_I = 8, 23, 38, 53
Z_I = 68
MATS = 75
N_SEMS = 99

BEFORE, BETWEEN = (0, 1), (2, 3, 4, 5, 8, 9)

PLANE = sorted(
    ((dx, dy) for dx in range(4) for dy in range(4) if dx or dy),
    key=lambda step: -sum(min(d, 4 - d) for d in step),
)
COLUMN = [(dz, d) for d in (2, 1, 3, 0) for dz in (1, 0) if dz or d]


def tables():
    n = np.arange(SIDE)
    angle = 2.0 * math.pi * (n[:, None] * n[None, :] % SIDE) / SIDE
    cosine = np.cos(angle) / math.sqrt(SIDE)
    sine = np.sin(angle) / math.sqrt(SIDE)
    first = np.block([[cosine, sine], [-sine, cosine]])
    return np.stack([first, first.T]).astype(BF)


def sin_cos(value):
    turns = jnp.floor(value * (2.0 / math.pi) + 0.5)
    rest = value - turns * 1.5703125
    rest = rest - turns * 4.837512969970703125e-4
    rest = rest - turns * 7.54978995489188216e-8
    square = rest * rest
    sine = ((-1.9515295891e-4 * square + 8.3321608736e-3) * square - 1.6666654611e-1) * square * rest + rest
    cosine = ((2.443315711809948e-5 * square - 1.388731625493765e-3) * square + 4.166664568298827e-2) * square * square
    cosine = cosine - 0.5 * square + 1.0
    quadrant = turns.astype(jnp.int32)
    odd = (quadrant & 1) == 1
    flip_sine = (quadrant & 2) == 2
    flip_cosine = ((quadrant + 1) & 2) == 2
    s = jnp.where(odd, cosine, sine)
    c = jnp.where(odd, sine, cosine)
    return jnp.where(flip_sine, -s, s), jnp.where(flip_cosine, -c, c)


def dot(left, right):
    return jnp.dot(left, right, preferred_element_type=F32)


def kernel(
    offset_ref,
    count_ref,
    position_ref,
    volume_hbm,
    matrix_hbm,
    measured_hbm,
    probe_hbm,
    table_hbm,
    windows_out,
    matrices,
    volume,
    matrix,
    measured,
    probe,
    table,
    offsets,
    tile_pad,
    grad_pad,
    s1,
    r1,
    acc1,
    s2,
    r2,
    sz,
    rz,
    full,
    window,
    t1,
    q1,
    acc2,
    t2,
    q2,
    zs,
    zr,
    slabs,
    load_sem,
    ssem,
    rsem,
):
    vx, y, s = lax.axis_index("vx"), lax.axis_index("vy"), lax.axis_index("scan")
    zl, x, c = vx // 8, (vx // 2) % 4, vx % 2

    def at(zl=zl, x=x, c=c, y=y, s=s):
        return (zl * 8 + x * 2 + c, y, s)

    def turn(index, d):
        return lax.rem(index + d, 4)

    def remote(number, src, dst, device):
        return pltpu.make_async_remote_copy(
            src_ref=src,
            dst_ref=dst,
            send_sem=ssem.at[number],
            recv_sem=rsem.at[number],
            device_id=device,
            device_id_type=MESH,
        )

    loads = [
        pltpu.make_async_copy(src, dst, load_sem.at[i])
        for i, (src, dst) in enumerate(
            [
                (volume_hbm, volume),
                (matrix_hbm, matrix),
                (measured_hbm, measured),
                (probe_hbm, probe),
                (table_hbm, table),
            ]
        )
    ]
    for load in loads:
        load.start()

    across = at(c=1 - c)
    plane = [at(x=turn(x, dx), y=turn(y, dy)) for dx, dy in PLANE]
    column = [at(zl=lax.rem(zl + dz, 2), s=turn(s, d)) for dz, d in COLUMN]
    barrier = pltpu.get_barrier_semaphore()
    for partner in [*column, *plane, across]:
        pl.semaphore_signal(barrier, inc=1, device_id=partner, device_id_type=MESH)

    for t in range(2):
        tile_pad[t, :, 0:384, :] = jnp.zeros((4, 384, 128), F32)
        tile_pad[t, :, 512:896, :] = jnp.zeros((4, 384, 128), F32)
    for k in range(CAP):
        grad_pad[k, :, 0:256, :] = jnp.zeros((4, 256, 128), F32)
        grad_pad[k, :, 512:768, :] = jnp.zeros((4, 256, 128), F32)
    for t in range(2):
        offsets[0, t] = jnp.full((8, 128), offset_ref[0, 0, t], jnp.int32)

    loads[0].wait()
    loads[1].wait()
    for t in range(2):
        for part in range(2):
            block = volume[part, :, 32 * t : 32 * t + 32, :].reshape(1024, 256)
            shadow = lax.dot_general(
                matrix[t], block, (((0,), (0,)), ((), ())), preferred_element_type=F32
            )
            for j in range(2):
                tile_pad[t, 2 * part + j, 384:512, :] = shadow[:, 128 * j : 128 * j + 128]

    def placed(padded, starts, h):
        blocks = []
        for j in range(2):
            terms = [padded[i, 2 * h + j, pl.ds(start, 256), :] for i, start in enumerate(starts)]
            blocks.append(functools.reduce(jnp.add, terms))
        return jnp.concatenate(blocks, axis=1).reshape(4, 4, 16, 256)

    def placed_tiles(h, first):
        return placed(tile_pad, [384 - offset_ref[0, 0, t] + first for t in range(2)], h)

    def reduced(source, s1, r1, core_number, acc, s2, r2, numbers):
        copy = remote(core_number, s1, r1, across)
        copy.start()
        sent.append(copy)
        for h in range(2):
            acc[:, :, h] = source(h, c * 256)
        copy.wait_recv()
        value = acc[...] + r1[...].astype(F32)
        acc[...] = value
        s2[...] = value.astype(BF)
        copies = []
        for i, (dx, dy) in enumerate(PLANE):
            copy = remote(numbers + i, s2.at[turn(x, dx), turn(y, dy)], r2.at[i], plane[i])
            copy.start()
            copies.append(copy)
        sent.extend(copies)
        value = acc[x, y]
        for copy in copies:
            copy.wait_recv()
        for i in range(len(PLANE)):
            value = value + r2[i].astype(F32)
        return value

    def gathered(whole, numbers, core_number):
        copies = []
        block = whole.at[c, x, y]
        for i in range(len(PLANE)):
            copy = remote(numbers + i, block, block, plane[i])
            copy.start()
            copies.append(copy)
        sent.extend(copies)
        for copy in copies:
            copy.wait_recv()
        block = whole.at[c]
        copy = remote(core_number, block, block, across)
        copy.start()
        sent.append(copy)
        copy.wait_recv()

    for h in range(2):
        s1[:, :, h] = placed_tiles(h, (1 - c) * 256).astype(BF)

    pl.semaphore_wait(barrier, 1 + len(PLANE) + len(COLUMN))
    sent = []
    right, left = at(s=turn(s, 1)), at(s=turn(s, 3))
    steps = []
    for i in range(12):
        t, quarter = (0, 0, 1)[i // 4], pl.ds(256 * (i % 4), 256)
        for j, device in enumerate((right, left)):
            tile = t if j == 0 else 1 - t
            own = matrix_hbm.at[tile, quarter]
            there = matrices.at[2 - 2 * j, tile, quarter]
            if i // 4 == 1:
                own, there = there, matrices.at[1, tile, quarter]
            steps.append(remote(MATS + 2 * i + j, own, there, device))
    arrived = set()

    def go(wanted):
        for i in wanted:
            for j in range(2):
                if i // 4 == 1:
                    steps[2 * (i - 4) + j].wait_recv()
                    arrived.add(2 * (i - 4) + j)
                steps[2 * i + j].start()

    early = []
    for d in (1, 2, 3):
        copy = remote(OFFS + d - 1, offsets.at[0], offsets.at[4 - d], at(s=turn(s, d)))
        early.append(copy)

    for copy in early:
        copy.start()
    go(BEFORE)
    block = reduced(placed_tiles, s1, r1, CORE_P, acc1, s2, r2, RS_P)
    sz[...] = block
    copy = remote(Z_P, sz, rz, at(zl=1 - zl))
    copy.start()
    sent.append(copy)
    copy.wait_recv()
    go(BETWEEN)
    full[c, x, y] = (block + rz[...]).astype(BF)
    gathered(full, AG_P, CORE_GP)
    for h in range(2):
        projection = full[:, :, :, h].reshape(512, 256).astype(F32)
        for j in range(2):
            window[h, j] = projection[:, 128 * j : 128 * j + 128]

    for load in loads[2:]:
        load.wait()
    lane = lax.broadcasted_iota(jnp.int32, (256, 128), 1)
    for k in range(CAP):
        rows = pl.ds(position_ref[0, 0, 0, k], 256)
        phase, loss = (
            jnp.concatenate([window[part, j, rows, :] for j in range(2)], axis=1) for part in range(2)
        )
        sine, cosine = sin_cos(phase)
        amplitude = jnp.exp(-ABSORPTION * loss)
        cosine, sine = amplitude * cosine, amplitude * sine
        exit_re = probe[0] * cosine - probe[1] * sine
        exit_im = probe[0] * sine + probe[1] * cosine

        half = dot(table[0], jnp.concatenate([exit_re, exit_im], axis=0).astype(BF)).astype(BF)
        far = dot(jnp.concatenate([half[:256], half[256:]], axis=1), table[1])
        far_re, far_im = far[:, :256], far[:, 256:]
        residue = 4.0 * (far_re * far_re + far_im * far_im - measured[k])
        residue_far = jnp.concatenate([residue * far_re, residue * far_im], axis=0).astype(BF)
        back = dot(table[1], residue_far).astype(BF)
        grad = dot(jnp.concatenate([back[:256], back[256:]], axis=1), table[0])
        grad_re, grad_im = grad[:, :256], grad[:, 256:]
        live = k < count_ref[0, 0]
        by_phase = jnp.where(live, grad_im * exit_re - grad_re * exit_im, 0.0)
        by_loss = jnp.where(live, -ABSORPTION * (grad_re * exit_re + grad_im * exit_im), 0.0)
        for h in range(2):
            a, b = by_phase[:, 128 * h : 128 * h + 128], by_loss[:, 128 * h : 128 * h + 128]
            even = jnp.where(lane < 64, a, pltpu.roll(b, 64, 1))
            odd = jnp.where(lane < 64, pltpu.roll(a, 64, 1), b)
            grad_pad[k, 2 * h, 256:512, :] = even
            grad_pad[k, 2 * h + 1, 256:512, :] = odd

    def placed_patches(h, first):
        return placed(grad_pad, [256 - position_ref[0, 0, 0, k] + first for k in range(CAP)], h)

    for h in range(2):
        t1[:, :, h] = placed_patches(h, (1 - c) * 256).astype(BF)
    block = reduced(placed_patches, t1, q1, CORE_I, acc2, t2, q2, RS_I)
    for k in range(4):
        zs[k] = block[k // 2, :, 128 * (k % 2) : 128 * (k % 2) + 128]
    zr[0, 0] = zs[s]
    copies = []
    for i, (dz, d) in enumerate(COLUMN):
        copy = remote(Z_I + i, zs.at[turn(s, d)], zr.at[dz, (4 - d) % 4], column[i])
        copy.start()
        copies.append(copy)
    sent.extend(copies)
    for copy in copies:
        copy.wait_recv()
    go([i for i in range(12) if i not in BEFORE and i not in BETWEEN])
    slabs[c, x, y] = (zr[0] + zr[1]).astype(BF)
    gathered(slabs, AG_I, CORE_GI)

    for copy in early:
        copy.wait_recv()
    columns = lax.broadcasted_iota(jnp.int32, (128, 512), 1) - lax.broadcasted_iota(jnp.int32, (128, 512), 0)
    for k in range(4):
        slab = slabs[:, :, :, k].reshape(512, 128)
        for t in range(2):
            first = jnp.broadcast_to(offsets[k, t][0:1, 0:1], (128, 512))
            chosen = jnp.where(columns == first, 1.0, 0.0).astype(BF)
            windows_out[t, 128 * k : 128 * k + 128, :] = dot(chosen, slab).astype(BF)
    for i, copy in enumerate(steps):
        if i not in arrived:
            copy.wait_recv()
    for copy in sent + early + steps:
        copy.wait_send()


def back_kernel(windows_hbm, own_hbm, matrices_hbm, out_hbm, windows, weights, out, load_sem, store_sem):
    loads = [pltpu.make_async_copy(windows_hbm, windows, load_sem.at[4])]
    for t in range(2):
        loads += [
            pltpu.make_async_copy(own_hbm.at[t], weights.at[t, 0], load_sem.at[2 * t]),
            pltpu.make_async_copy(matrices_hbm.at[:, t], weights.at[t, pl.ds(1, 3)], load_sem.at[2 * t + 1]),
        ]
    for load in loads:
        load.start()
    for load in loads:
        load.wait()
    stores = []
    for quarter in range(4):
        lines = pl.ds(8 * quarter, 8)
        for t in range(2):
            side = jnp.concatenate([weights[t, k, 256 * quarter : 256 * quarter + 256] for k in range(4)], axis=1)
            slope = (-STEP_LENGTH * dot(side, windows[t])).reshape(8, 32, 128)
            for part in range(2):
                out[part, lines, 32 * t : 32 * t + 32, :] = slope[:, :, 64 * part : 64 * part + 64]
        for part in range(2):
            store = pltpu.make_async_copy(
                out.at[part, lines], out_hbm.at[part, lines], store_sem.at[2 * quarter + part]
            )
            store.start()
            stores.append(store)
    for store in stores:
        store.wait()


def per_device(volume, tile_matrix, tile_offset, patch_count, scan_position, measured, illumination):
    any_space = pl.BlockSpec(memory_space=pl.ANY)
    smem = pl.BlockSpec(memory_space=pltpu.SMEM)
    block = (4, 4, 2, 16, 256)
    tile_matrix = tile_matrix.reshape(2, 1024, 128)
    windows, matrices = pl.pallas_call(
        kernel,
        out_shape=(
            jax.ShapeDtypeStruct((2, 512, 128), BF),
            jax.ShapeDtypeStruct((3, 2, 1024, 128), BF),
        ),
        in_specs=[smem] * 3 + [any_space] * 5,
        out_specs=(pl.BlockSpec(memory_space=pltpu.VMEM), any_space),
        scratch_shapes=[
            pltpu.VMEM((2, 32, 64, 256), BF),
            pltpu.VMEM((2, 1024, 128), BF),
            pltpu.VMEM((3, 256, 256), F32),
            pltpu.VMEM((2, 256, 256), F32),
            pltpu.VMEM((2, 512, 512), BF),
            pltpu.VMEM((4, 2, 8, 128), jnp.int32),
            pltpu.VMEM((2, 4, 896, 128), F32),
            pltpu.VMEM((3, 4, 768, 128), F32),
            pltpu.VMEM(block, BF),
            pltpu.VMEM(block, BF),
            pltpu.VMEM(block, F32),
            pltpu.VMEM(block, BF),
            pltpu.VMEM((15, 2, 16, 256), BF),
            pltpu.VMEM((2, 16, 256), F32),
            pltpu.VMEM((2, 16, 256), F32),
            pltpu.VMEM((2, *block), BF),
            pltpu.VMEM((2, 2, 512, 128), F32),
            pltpu.VMEM(block, BF),
            pltpu.VMEM(block, BF),
            pltpu.VMEM(block, F32),
            pltpu.VMEM(block, BF),
            pltpu.VMEM((15, 2, 16, 256), BF),
            pltpu.VMEM((4, 16, 128), F32),
            pltpu.VMEM((2, 4, 16, 128), F32),
            pltpu.VMEM((2, 4, 4, 4, 16, 128), BF),
            pltpu.SemaphoreType.DMA((5,)),
            pltpu.SemaphoreType.DMA((N_SEMS,)),
            pltpu.SemaphoreType.DMA((N_SEMS,)),
        ],
        compiler_params=pltpu.CompilerParams(
            collective_id=0, has_side_effects=True, vmem_limit_bytes=60 * 2**20
        ),
    )(
        tile_offset,
        patch_count,
        jnp.swapaxes(scan_position, 2, 3),
        volume,
        tile_matrix,
        measured.reshape(3, 256, 256),
        illumination,
        jnp.asarray(tables()),
    )
    return pl.pallas_call(
        back_kernel,
        out_shape=jax.ShapeDtypeStruct((2, 32, 64, 64), F32),
        in_specs=[any_space] * 3,
        out_specs=any_space,
        scratch_shapes=[
            pltpu.VMEM((2, 512, 128), BF),
            pltpu.VMEM((2, 4, 1024, 128), BF),
            pltpu.VMEM((2, 32, 64, 64), F32),
            pltpu.SemaphoreType.DMA((5,)),
            pltpu.SemaphoreType.DMA((8,)),
        ],
        compiler_params=pltpu.CompilerParams(vmem_limit_bytes=60 * 2**20),
    )(windows, tile_matrix, matrices)


def solution(mesh):
    in_specs = (
        P(None, "vx", "vy", None),
        P("scan", "vx", "vy", None, None),
        P("scan", "vx", "vy"),
        P("scan", ("vx", "vy")),
        P("scan", ("vx", "vy"), None, None),
        P("scan", ("vx", "vy"), None, None, None),
        P(),
    )
    out_specs = P(None, "vx", "vy", "scan")
    return jax.shard_map(
        per_device, mesh=mesh, in_specs=in_specs, out_specs=out_specs, check_vma=False
    )
```

```python
import functools
import math

import jax
import jax.numpy as jnp
import numpy as np
from jax import lax
from jax.experimental import pallas as pl
from jax.experimental.pallas import tpu as pltpu
from jax.sharding import PartitionSpec as P

MESH = pl.DeviceIdType.MESH
BF = jnp.bfloat16
F32 = jnp.float32

ABSORPTION = 0.2
STEP_LENGTH = 0.003
SIDE = 256
CAP = 3

CORE_P, CORE_I, CORE_GP, CORE_GI = 0, 4, 8, 12
Z_P = 16
OFFS = 17
RS_P, RS_I, AG_P, AG_I = 20, 35, 50, 65
Z_I = 80
MATS = 87
N_SEMS = 111

BEFORE, BETWEEN = (0, 1), (2, 3, 4, 5, 8, 9)

ROWS = (2, 1, 3, 0)
PLANE = [(dx, dy) for dx in ROWS for dy in (2, 1, 3, 0) if dx or dy]
COLUMN = [(dz, d) for d in (2, 1, 3, 0) for dz in (1, 0) if dz or d]


def tables():
    n = np.arange(SIDE)
    angle = 2.0 * math.pi * (n[:, None] * n[None, :] % SIDE) / SIDE
    cosine = np.cos(angle) / math.sqrt(SIDE)
    sine = np.sin(angle) / math.sqrt(SIDE)
    first = np.block([[cosine, sine], [-sine, cosine]])
    return np.stack([first, first.T]).astype(BF)


def sin_cos(value):
    turns = jnp.floor(value * (2.0 / math.pi) + 0.5)
    rest = value - turns * 1.5703125
    rest = rest - turns * 4.837512969970703125e-4
    rest = rest - turns * 7.54978995489188216e-8
    square = rest * rest
    sine = ((-1.9515295891e-4 * square + 8.3321608736e-3) * square - 1.6666654611e-1) * square * rest + rest
    cosine = ((2.443315711809948e-5 * square - 1.388731625493765e-3) * square + 4.166664568298827e-2) * square * square
    cosine = cosine - 0.5 * square + 1.0
    quadrant = turns.astype(jnp.int32)
    odd = (quadrant & 1) == 1
    flip_sine = (quadrant & 2) == 2
    flip_cosine = ((quadrant + 1) & 2) == 2
    s = jnp.where(odd, cosine, sine)
    c = jnp.where(odd, sine, cosine)
    return jnp.where(flip_sine, -s, s), jnp.where(flip_cosine, -c, c)


def dot(left, right):
    return jnp.dot(left, right, preferred_element_type=F32)


def kernel(
    offset_ref,
    count_ref,
    position_ref,
    volume_hbm,
    matrix_hbm,
    measured_hbm,
    probe_hbm,
    table_hbm,
    windows_out,
    matrices,
    volume,
    measured,
    probe,
    table,
    offsets,
    tile_pad,
    grad_pad,
    s1,
    r1,
    acc1,
    s2,
    r2,
    sz,
    rz,
    full,
    window,
    t1,
    q1,
    acc2,
    t2,
    q2,
    zs,
    zr,
    slabs,
    picks,
    own_rows,
    load_sem,
    ssem,
    rsem,
):
    vx, y, s = lax.axis_index("vx"), lax.axis_index("vy"), lax.axis_index("scan")
    zl, x, c = vx // 8, (vx // 2) % 4, vx % 2

    def at(zl=zl, x=x, c=c, y=y, s=s):
        return (zl * 8 + x * 2 + c, y, s)

    def turn(index, d):
        return lax.rem(index + d, 4)

    def remote(number, src, dst, device):
        return pltpu.make_async_remote_copy(
            src_ref=src,
            dst_ref=dst,
            send_sem=ssem.at[number],
            recv_sem=rsem.at[number],
            device_id=device,
            device_id_type=MESH,
        )

    loads = [
        pltpu.make_async_copy(src, dst, load_sem.at[i])
        for i, (src, dst) in enumerate(
            [
                (volume_hbm, volume),
                (matrix_hbm, matrices.at[0]),
                (measured_hbm, measured),
                (probe_hbm, probe),
                (table_hbm, table),
            ]
        )
    ]
    for load in loads:
        load.start()

    across = at(c=1 - c)
    plane = [at(x=turn(x, dx), y=turn(y, dy)) for dx, dy in PLANE]
    column = [at(zl=lax.rem(zl + dz, 2), s=turn(s, d)) for dz, d in COLUMN]
    barrier = pltpu.get_barrier_semaphore()
    for partner in [*column, *plane, across]:
        pl.semaphore_signal(barrier, inc=1, device_id=partner, device_id_type=MESH)

    for t in range(2):
        tile_pad[t, :, 0:384, :] = jnp.zeros((4, 384, 128), F32)
        tile_pad[t, :, 512:896, :] = jnp.zeros((4, 384, 128), F32)
    for k in range(CAP):
        grad_pad[k, :, 0:256, :] = jnp.zeros((4, 256, 128), F32)
        grad_pad[k, :, 512:768, :] = jnp.zeros((4, 256, 128), F32)
    for t in range(2):
        offsets[0, t] = jnp.full((8, 128), offset_ref[0, 0, t], jnp.int32)

    loads[0].wait()
    loads[1].wait()
    for t in range(2):
        for part in range(2):
            block = volume[part, :, 32 * t : 32 * t + 32, :].reshape(1024, 256)
            shadow = lax.dot_general(
                matrices[0, t], block, (((0,), (0,)), ((), ())), preferred_element_type=F32
            )
            for j in range(2):
                tile_pad[t, 2 * part + j, 384:512, :] = shadow[:, 128 * j : 128 * j + 128]

    def placed(padded, starts, h):
        blocks = []
        for j in range(2):
            terms = [padded[i, 2 * h + j, pl.ds(start, 64), :] for i, start in enumerate(starts)]
            blocks.append(functools.reduce(jnp.add, terms))
        return jnp.concatenate(blocks, axis=1).reshape(4, 16, 256)

    def placed_tiles(h, first):
        return placed(tile_pad, [384 - offset_ref[0, 0, t] + first for t in range(2)], h)

    def fill(source, s1, row):
        for h in range(2):
            s1[row, :, h] = source(h, (1 - c) * 256 + row * 64).astype(BF)

    def reduced(source, filled, s1, r1, core_number, acc, s2, r2, numbers, beside):
        swaps = []
        for g, dx in enumerate(ROWS):
            row = turn(x, dx)
            if not filled:
                fill(source, s1, row)
            copy = remote(core_number + g, s1.at[row], r1.at[row], across)
            copy.start()
            swaps.append(copy)
        beside()
        for dx in ROWS:
            row = turn(x, dx)
            for h in range(2):
                acc[row, :, h] = source(h, c * 256 + row * 64)
        copies = []
        for g, dx in enumerate(ROWS):
            row = turn(x, dx)
            swaps[g].wait_recv()
            value = acc[row] + r1[row].astype(F32)
            acc[row] = value
            s2[row] = value.astype(BF)
            for i, (ex, dy) in enumerate(PLANE):
                if ex == dx:
                    copy = remote(numbers + i, s2.at[row, turn(y, dy)], r2.at[i], plane[i])
                    copy.start()
                    copies.append(copy)
        sent.extend(swaps + copies)
        value = acc[x, y]
        for copy in copies:
            copy.wait_recv()
        for i in range(len(PLANE)):
            value = value + r2[i].astype(F32)
        return value

    def gathered(whole, numbers, core_number, beside, use):
        copies = []
        block = whole.at[c, x, y]
        for i in range(len(PLANE)):
            copy = remote(numbers + i, block, block, plane[i])
            copy.start()
            copies.append(copy)
        beside()
        swaps = []
        for g, dx in enumerate(ROWS[::-1]):
            for i, (ex, dy) in enumerate(PLANE):
                if ex == dx:
                    copies[i].wait_recv()
            block = whole.at[c, turn(x, 4 - dx)]
            copy = remote(core_number + g, block, block, across)
            copy.start()
            swaps.append(copy)
        sent.extend(copies + swaps)
        use(0)
        for copy in swaps:
            copy.wait_recv()
        use(1)

    for dx in ROWS:
        fill(placed_tiles, s1, turn(x, dx))

    pl.semaphore_wait(barrier, 1 + len(PLANE) + len(COLUMN))
    sent = []
    right, left = at(s=turn(s, 1)), at(s=turn(s, 3))
    steps = []
    for i in range(12):
        t, quarter = (0, 0, 1)[i // 4], pl.ds(256 * (i % 4), 256)
        for j, device in enumerate((right, left)):
            tile = t if j == 0 else 1 - t
            own = matrix_hbm.at[tile, quarter]
            there = matrices.at[3 - 2 * j, tile, quarter]
            if i // 4 == 1:
                own, there = there, matrices.at[2, tile, quarter]
            steps.append(remote(MATS + 2 * i + j, own, there, device))
    arrived = set()

    def go(wanted):
        for i in wanted:
            for j in range(2):
                if i // 4 == 1:
                    steps[2 * (i - 4) + j].wait_recv()
                    arrived.add(2 * (i - 4) + j)
                steps[2 * i + j].start()

    early = []
    for d in (1, 2, 3):
        copy = remote(OFFS + d - 1, offsets.at[0], offsets.at[4 - d], at(s=turn(s, d)))
        early.append(copy)

    def beside_first():
        for copy in early:
            copy.start()
        go(BEFORE)

    def widen(other):
        half = c if other == 0 else 1 - c
        for h in range(2):
            projection = full[half, :, :, h].reshape(256, 256).astype(F32)
            for j in range(2):
                window[h, j, pl.ds(half * 256, 256), :] = projection[:, 128 * j : 128 * j + 128]

    block = reduced(placed_tiles, True, s1, r1, CORE_P, acc1, s2, r2, RS_P, beside_first)
    sz[...] = block
    copy = remote(Z_P, sz, rz, at(zl=1 - zl))
    copy.start()
    sent.append(copy)
    copy.wait_recv()
    full[c, x, y] = (block + rz[...]).astype(BF)
    gathered(full, AG_P, CORE_GP, lambda: go(BETWEEN), widen)

    for load in loads[2:]:
        load.wait()
    lane = lax.broadcasted_iota(jnp.int32, (256, 128), 1)
    for k in range(CAP):
        rows = pl.ds(position_ref[0, 0, 0, k], 256)
        phase, loss = (
            jnp.concatenate([window[part, j, rows, :] for j in range(2)], axis=1) for part in range(2)
        )
        sine, cosine = sin_cos(phase)
        amplitude = jnp.exp(-ABSORPTION * loss)
        cosine, sine = amplitude * cosine, amplitude * sine
        exit_re = probe[0] * cosine - probe[1] * sine
        exit_im = probe[0] * sine + probe[1] * cosine

        half = dot(table[0], jnp.concatenate([exit_re, exit_im], axis=0).astype(BF)).astype(BF)
        far = dot(jnp.concatenate([half[:256], half[256:]], axis=1), table[1])
        far_re, far_im = far[:, :256], far[:, 256:]
        residue = 4.0 * (far_re * far_re + far_im * far_im - measured[k])
        residue_far = jnp.concatenate([residue * far_re, residue * far_im], axis=0).astype(BF)
        back = dot(table[1], residue_far).astype(BF)
        grad = dot(jnp.concatenate([back[:256], back[256:]], axis=1), table[0])
        grad_re, grad_im = grad[:, :256], grad[:, 256:]
        live = k < count_ref[0, 0]
        by_phase = jnp.where(live, grad_im * exit_re - grad_re * exit_im, 0.0)
        by_loss = jnp.where(live, -ABSORPTION * (grad_re * exit_re + grad_im * exit_im), 0.0)
        for h in range(2):
            a, b = by_phase[:, 128 * h : 128 * h + 128], by_loss[:, 128 * h : 128 * h + 128]
            even = jnp.where(lane < 64, a, pltpu.roll(b, 64, 1))
            odd = jnp.where(lane < 64, pltpu.roll(a, 64, 1), b)
            grad_pad[k, 2 * h, 256:512, :] = even
            grad_pad[k, 2 * h + 1, 256:512, :] = odd

    def placed_patches(h, first):
        return placed(grad_pad, [256 - position_ref[0, 0, 0, k] + first for k in range(CAP)], h)

    block = reduced(placed_patches, False, t1, q1, CORE_I, acc2, t2, q2, RS_I, lambda: None)
    for k in range(4):
        zs[k] = block[k // 2, :, 128 * (k % 2) : 128 * (k % 2) + 128]
    zr[0, 0] = zs[s]
    copies = []
    for i, (dz, d) in enumerate(COLUMN):
        copy = remote(Z_I + i, zs.at[turn(s, d)], zr.at[dz, (4 - d) % 4], column[i])
        copy.start()
        copies.append(copy)
    sent.extend(copies)
    for copy in copies:
        copy.wait_recv()
    slabs[c, x, y] = (zr[0] + zr[1]).astype(BF)

    def beside_last():
        go([i for i in range(12) if i not in BEFORE and i not in BETWEEN])
        for copy in early:
            copy.wait_recv()
        distance = lax.broadcasted_iota(jnp.int32, (128, 256), 1) - lax.broadcasted_iota(jnp.int32, (128, 256), 0)
        for other in range(2):
            rows = distance + 256 * (c if other == 0 else 1 - c)
            for k in range(4):
                for t in range(2):
                    first = jnp.broadcast_to(offsets[k, t][0:1, 0:1], (128, 256))
                    picks[other, k, t] = jnp.where(rows == first, 1.0, 0.0).astype(BF)

    def picked(other):
        half = c if other == 0 else 1 - c
        for k in range(4):
            slab = slabs[half, :, :, k].reshape(256, 128)
            for t in range(2):
                value = dot(picks[other, k, t], slab)
                if other == 0:
                    own_rows[k, t] = value
                else:
                    windows_out[t, 128 * k : 128 * k + 128, :] = (own_rows[k, t] + value).astype(BF)

    gathered(slabs, AG_I, CORE_GI, beside_last, picked)
    for i, copy in enumerate(steps):
        if i not in arrived:
            copy.wait_recv()
    for copy in sent + early + steps:
        copy.wait_send()


def back_kernel(windows, matrices, out_hbm, out, store_sem):
    stores = []
    for quarter in range(4):
        lines = pl.ds(8 * quarter, 8)
        for t in range(2):
            rows = pl.ds(256 * quarter, 256)
            side = jnp.concatenate([matrices[k, t, rows] for k in range(4)], axis=1)
            slope = (-STEP_LENGTH * dot(side, windows[t])).reshape(8, 32, 128)
            for part in range(2):
                out[part, lines, 32 * t : 32 * t + 32, :] = slope[:, :, 64 * part : 64 * part + 64]
        for part in range(2):
            store = pltpu.make_async_copy(
                out.at[part, lines], out_hbm.at[part, lines], store_sem.at[2 * quarter + part]
            )
            store.start()
            stores.append(store)
    for store in stores:
        store.wait()


def per_device(volume, tile_matrix, tile_offset, patch_count, scan_position, measured, illumination):
    any_space = pl.BlockSpec(memory_space=pl.ANY)
    vmem = pl.BlockSpec(memory_space=pltpu.VMEM)
    smem = pl.BlockSpec(memory_space=pltpu.SMEM)
    block = (4, 4, 2, 16, 256)
    tile_matrix = tile_matrix.reshape(2, 1024, 128)
    arrays = (volume, tile_matrix, measured.reshape(3, 256, 256), illumination, jnp.asarray(tables()))
    windows, matrices = pl.pallas_call(
        kernel,
        out_shape=(
            pltpu.VMEM((2, 512, 128), BF),
            pltpu.VMEM((4, 2, 1024, 128), BF),
        ),
        in_specs=[smem] * 3 + [any_space] * 5,
        out_specs=(vmem, vmem),
        scratch_shapes=[
            pltpu.VMEM((2, 32, 64, 256), BF),
            pltpu.VMEM((3, 256, 256), F32),
            pltpu.VMEM((2, 256, 256), F32),
            pltpu.VMEM((2, 512, 512), BF),
            pltpu.VMEM((4, 2, 8, 128), jnp.int32),
            pltpu.VMEM((2, 4, 896, 128), F32),
            pltpu.VMEM((3, 4, 768, 128), F32),
            pltpu.VMEM(block, BF),
            pltpu.VMEM(block, BF),
            pltpu.VMEM(block, F32),
            pltpu.VMEM(block, BF),
            pltpu.VMEM((15, 2, 16, 256), BF),
            pltpu.VMEM((2, 16, 256), F32),
            pltpu.VMEM((2, 16, 256), F32),
            pltpu.VMEM((2, *block), BF),
            pltpu.VMEM((2, 2, 512, 128), F32),
            pltpu.VMEM(block, BF),
            pltpu.VMEM(block, BF),
            pltpu.VMEM(block, F32),
            pltpu.VMEM(block, BF),
            pltpu.VMEM((15, 2, 16, 256), BF),
            pltpu.VMEM((4, 16, 128), F32),
            pltpu.VMEM((2, 4, 16, 128), F32),
            pltpu.VMEM((2, 4, 4, 4, 16, 128), BF),
            pltpu.VMEM((2, 4, 2, 128, 256), BF),
            pltpu.VMEM((4, 2, 128, 128), F32),
            pltpu.SemaphoreType.DMA((5,)),
            pltpu.SemaphoreType.DMA((N_SEMS,)),
            pltpu.SemaphoreType.DMA((N_SEMS,)),
        ],
        compiler_params=pltpu.CompilerParams(
            collective_id=0, has_side_effects=True, vmem_limit_bytes=44 * 2**20
        ),
    )(
        pltpu.with_memory_space_constraint(tile_offset, pltpu.HBM),
        patch_count,
        pltpu.with_memory_space_constraint(jnp.swapaxes(scan_position, 2, 3), pltpu.HBM),
        *(pltpu.with_memory_space_constraint(a, pltpu.HBM) for a in arrays),
    )
    return pl.pallas_call(
        back_kernel,
        out_shape=jax.ShapeDtypeStruct((2, 32, 64, 64), F32),
        in_specs=[vmem, vmem],
        out_specs=any_space,
        scratch_shapes=[
            pltpu.VMEM((2, 32, 64, 64), F32),
            pltpu.SemaphoreType.DMA((8,)),
        ],
        compiler_params=pltpu.CompilerParams(vmem_limit_bytes=44 * 2**20),
    )(*(pltpu.with_memory_space_constraint(a, pltpu.VMEM) for a in (windows, matrices)))


def solution(mesh):
    in_specs = (
        P(None, "vx", "vy", None),
        P("scan", "vx", "vy", None, None),
        P("scan", "vx", "vy"),
        P("scan", ("vx", "vy")),
        P("scan", ("vx", "vy"), None, None),
        P("scan", ("vx", "vy"), None, None, None),
        P(),
    )
    out_specs = P(None, "vx", "vy", "scan")
    return jax.shard_map(
        per_device, mesh=mesh, in_specs=in_specs, out_specs=out_specs, check_vma=False
    )
```

```python
import functools
import math

import jax
import jax.numpy as jnp
import numpy as np
from jax import lax
from jax.experimental import pallas as pl
from jax.experimental.pallas import tpu as pltpu
from jax.sharding import PartitionSpec as P

MESH = pl.DeviceIdType.MESH
BF = jnp.bfloat16
F32 = jnp.float32

ABSORPTION = 0.2
STEP_LENGTH = 0.003
SIDE = 256
CAP = 3

CORE_P, CORE_I, CORE_GP, CORE_GI = 0, 4, 8, 12
Z_P = 16
OFFS = 17
RS_P, RS_I, AG_P, AG_I = 20, 35, 50, 65
Z_I = 80
MATS = 87
N_SEMS = 111

BEFORE, BETWEEN = (0, 1), (2, 3, 4, 5, 8, 9)

ROWS = (2, 1, 3, 0)
PLANE = [(dx, dy) for dx in ROWS for dy in (2, 1, 3, 0) if dx or dy]
COLUMN = [(dz, d) for d in (2, 1, 3, 0) for dz in (1, 0) if dz or d]


def tables():
    n = np.arange(SIDE)
    angle = 2.0 * math.pi * (n[:, None] * n[None, :] % SIDE) / SIDE
    cosine = np.cos(angle) / math.sqrt(SIDE)
    sine = np.sin(angle) / math.sqrt(SIDE)
    first = np.block([[cosine, sine], [-sine, cosine]])
    return np.stack([first, first.T]).astype(BF)


def sin_cos(value):
    turns = jnp.floor(value * (2.0 / math.pi) + 0.5)
    rest = value - turns * 1.5703125
    rest = rest - turns * 4.837512969970703125e-4
    rest = rest - turns * 7.54978995489188216e-8
    square = rest * rest
    sine = ((-1.9515295891e-4 * square + 8.3321608736e-3) * square - 1.6666654611e-1) * square * rest + rest
    cosine = ((2.443315711809948e-5 * square - 1.388731625493765e-3) * square + 4.166664568298827e-2) * square * square
    cosine = cosine - 0.5 * square + 1.0
    quadrant = turns.astype(jnp.int32)
    odd = (quadrant & 1) == 1
    flip_sine = (quadrant & 2) == 2
    flip_cosine = ((quadrant + 1) & 2) == 2
    s = jnp.where(odd, cosine, sine)
    c = jnp.where(odd, sine, cosine)
    return jnp.where(flip_sine, -s, s), jnp.where(flip_cosine, -c, c)


def dot(left, right):
    return jnp.dot(left, right, preferred_element_type=F32)


def kernel(
    offset_ref,
    count_ref,
    position_ref,
    volume_hbm,
    matrix_hbm,
    measured_hbm,
    probe_hbm,
    table_hbm,
    windows_out,
    matrices,
    volume,
    measured,
    probe,
    table,
    offsets,
    tile_pad,
    grad_pad,
    s1,
    r1,
    acc1,
    s2,
    r2,
    sz,
    rz,
    full,
    window,
    t1,
    q1,
    acc2,
    t2,
    q2,
    zs,
    zr,
    slabs,
    picks,
    own_rows,
    load_sem,
    ssem,
    rsem,
):
    vx, y, s = lax.axis_index("vx"), lax.axis_index("vy"), lax.axis_index("scan")
    zl, x, c = vx // 8, (vx // 2) % 4, vx % 2

    def at(zl=zl, x=x, c=c, y=y, s=s):
        return (zl * 8 + x * 2 + c, y, s)

    def turn(index, d):
        return lax.rem(index + d, 4)

    def remote(number, src, dst, device):
        return pltpu.make_async_remote_copy(
            src_ref=src,
            dst_ref=dst,
            send_sem=ssem.at[number],
            recv_sem=rsem.at[number],
            device_id=device,
            device_id_type=MESH,
        )

    loads = [
        pltpu.make_async_copy(src, dst, load_sem.at[i])
        for i, (src, dst) in enumerate(
            [
                (volume_hbm, volume),
                (matrix_hbm, matrices.at[0]),
                (measured_hbm, measured),
                (probe_hbm, probe),
                (table_hbm, table),
            ]
        )
    ]
    for load in loads:
        load.start()

    across = at(c=1 - c)
    plane = [at(x=turn(x, dx), y=turn(y, dy)) for dx, dy in PLANE]
    column = [at(zl=lax.rem(zl + dz, 2), s=turn(s, d)) for dz, d in COLUMN]
    barrier = pltpu.get_barrier_semaphore()
    for partner in [*column, *plane, across]:
        pl.semaphore_signal(barrier, inc=1, device_id=partner, device_id_type=MESH)

    for t in range(2):
        tile_pad[t, :, 0:384, :] = jnp.zeros((4, 384, 128), F32)
        tile_pad[t, :, 512:896, :] = jnp.zeros((4, 384, 128), F32)
    for k in range(CAP):
        grad_pad[k, :, 0:256, :] = jnp.zeros((4, 256, 128), F32)
        grad_pad[k, :, 512:768, :] = jnp.zeros((4, 256, 128), F32)
    for t in range(2):
        offsets[0, t] = jnp.full((8, 128), offset_ref[0, 0, t], jnp.int32)

    loads[0].wait()
    loads[1].wait()
    for t in range(2):
        for part in range(2):
            block = volume[part, :, 32 * t : 32 * t + 32, :].reshape(1024, 256)
            shadow = lax.dot_general(
                matrices[0, t], block, (((0,), (0,)), ((), ())), preferred_element_type=F32
            )
            for j in range(2):
                tile_pad[t, 2 * part + j, 384:512, :] = shadow[:, 128 * j : 128 * j + 128]

    def placed(padded, starts, h):
        blocks = []
        for j in range(2):
            terms = [padded[i, 2 * h + j, pl.ds(start, 64), :] for i, start in enumerate(starts)]
            blocks.append(functools.reduce(jnp.add, terms))
        return jnp.concatenate(blocks, axis=1).reshape(4, 16, 256)

    def placed_tiles(h, first):
        return placed(tile_pad, [384 - offset_ref[0, 0, t] + first for t in range(2)], h)

    def fill(source, s1, row):
        for h in range(2):
            s1[row, :, h] = source(h, (1 - c) * 256 + row * 64).astype(BF)

    def reduced(source, filled, s1, r1, core_number, acc, s2, r2, numbers, beside):
        swaps = []
        for g, dx in enumerate(ROWS):
            row = turn(x, dx)
            if not filled:
                fill(source, s1, row)
            copy = remote(core_number + g, s1.at[row], r1.at[row], across)
            copy.start()
            swaps.append(copy)
        beside()
        for dx in ROWS:
            row = turn(x, dx)
            for h in range(2):
                acc[row, :, h] = source(h, c * 256 + row * 64)
        copies = []
        for g, dx in enumerate(ROWS):
            row = turn(x, dx)
            swaps[g].wait_recv()
            value = acc[row] + r1[row].astype(F32)
            acc[row] = value
            s2[row] = value.astype(BF)
            for i, (ex, dy) in enumerate(PLANE):
                if ex == dx:
                    copy = remote(numbers + i, s2.at[row, turn(y, dy)], r2.at[i], plane[i])
                    copy.start()
                    copies.append(copy)
        sent.extend(swaps + copies)
        value = acc[x, y]
        for copy in copies:
            copy.wait_recv()
        for i in range(len(PLANE)):
            value = value + r2[i].astype(F32)
        return value

    def gathered(whole, numbers, core_number, beside, use):
        copies = []
        block = whole.at[c, x, y]
        for i in range(len(PLANE)):
            copy = remote(numbers + i, block, block, plane[i])
            copy.start()
            copies.append(copy)
        beside()
        swaps = []
        for g, dx in enumerate(ROWS[::-1]):
            for i, (ex, dy) in enumerate(PLANE):
                if ex == dx:
                    copies[i].wait_recv()
            block = whole.at[c, turn(x, 4 - dx)]
            copy = remote(core_number + g, block, block, across)
            copy.start()
            swaps.append(copy)
        sent.extend(copies + swaps)
        use(0)
        for copy in swaps:
            copy.wait_recv()
        use(1)

    for dx in ROWS:
        fill(placed_tiles, s1, turn(x, dx))

    pl.semaphore_wait(barrier, 1 + len(PLANE) + len(COLUMN))
    sent = []
    right, left = at(s=turn(s, 1)), at(s=turn(s, 3))
    steps = []
    for i in range(12):
        t, quarter = (0, 0, 1)[i // 4], pl.ds(256 * (i % 4), 256)
        for j, device in enumerate((right, left)):
            tile = t if j == 0 else 1 - t
            own = matrix_hbm.at[tile, quarter]
            there = matrices.at[3 - 2 * j, tile, quarter]
            if i // 4 == 1:
                own, there = there, matrices.at[2, tile, quarter]
            steps.append(remote(MATS + 2 * i + j, own, there, device))
    arrived = set()

    def go(wanted):
        for i in wanted:
            for j in range(2):
                if i // 4 == 1:
                    steps[2 * (i - 4) + j].wait_recv()
                    arrived.add(2 * (i - 4) + j)
                steps[2 * i + j].start()

    early = []
    for d in (1, 2, 3):
        copy = remote(OFFS + d - 1, offsets.at[0], offsets.at[4 - d], at(s=turn(s, d)))
        early.append(copy)

    def beside_first():
        for copy in early:
            copy.start()
        go(BEFORE)

    def widen(other):
        half = c if other == 0 else 1 - c
        for h in range(2):
            projection = full[half, :, :, h].reshape(256, 256).astype(F32)
            for j in range(2):
                window[h, j, pl.ds(half * 256, 256), :] = projection[:, 128 * j : 128 * j + 128]

    block = reduced(placed_tiles, True, s1, r1, CORE_P, acc1, s2, r2, RS_P, beside_first)
    sz[...] = block
    copy = remote(Z_P, sz, rz, at(zl=1 - zl))
    copy.start()
    sent.append(copy)
    copy.wait_recv()
    full[c, x, y] = (block + rz[...]).astype(BF)
    gathered(full, AG_P, CORE_GP, lambda: go(BETWEEN), widen)

    for load in loads[2:]:
        load.wait()
    lane = lax.broadcasted_iota(jnp.int32, (256, 128), 1)
    for k in range(CAP):
        rows = pl.ds(position_ref[0, 0, 0, k], 256)
        phase, loss = (
            jnp.concatenate([window[part, j, rows, :] for j in range(2)], axis=1) for part in range(2)
        )
        sine, cosine = sin_cos(phase)
        amplitude = jnp.exp(-ABSORPTION * loss)
        cosine, sine = amplitude * cosine, amplitude * sine
        exit_re = probe[0] * cosine - probe[1] * sine
        exit_im = probe[0] * sine + probe[1] * cosine

        half = dot(table[0], jnp.concatenate([exit_re, exit_im], axis=0).astype(BF)).astype(BF)
        far = dot(jnp.concatenate([half[:256], half[256:]], axis=1), table[1])
        far_re, far_im = far[:, :256], far[:, 256:]
        residue = 4.0 * (far_re * far_re + far_im * far_im - measured[k])
        residue_far = jnp.concatenate([residue * far_re, residue * far_im], axis=0).astype(BF)
        back = dot(table[1], residue_far).astype(BF)
        grad = dot(jnp.concatenate([back[:256], back[256:]], axis=1), table[0])
        grad_re, grad_im = grad[:, :256], grad[:, 256:]
        live = k < count_ref[0, 0]
        by_phase = jnp.where(live, grad_im * exit_re - grad_re * exit_im, 0.0)
        by_loss = jnp.where(live, -ABSORPTION * (grad_re * exit_re + grad_im * exit_im), 0.0)
        for h in range(2):
            a, b = by_phase[:, 128 * h : 128 * h + 128], by_loss[:, 128 * h : 128 * h + 128]
            even = jnp.where(lane < 64, a, pltpu.roll(b, 64, 1))
            odd = jnp.where(lane < 64, pltpu.roll(a, 64, 1), b)
            grad_pad[k, 2 * h, 256:512, :] = even
            grad_pad[k, 2 * h + 1, 256:512, :] = odd

    def placed_patches(h, first):
        return placed(grad_pad, [256 - position_ref[0, 0, 0, k] + first for k in range(CAP)], h)

    block = reduced(placed_patches, False, t1, q1, CORE_I, acc2, t2, q2, RS_I, lambda: None)
    for k in range(4):
        zs[k] = block[k // 2, :, 128 * (k % 2) : 128 * (k % 2) + 128]
    zr[0, 0] = zs[s]
    copies = []
    for i, (dz, d) in enumerate(COLUMN):
        copy = remote(Z_I + i, zs.at[turn(s, d)], zr.at[dz, (4 - d) % 4], column[i])
        copy.start()
        copies.append(copy)
    sent.extend(copies)
    go([i for i in range(12) if i not in BEFORE and i not in BETWEEN])
    for copy in copies:
        copy.wait_recv()
    slabs[c, x, y] = (zr[0] + zr[1]).astype(BF)

    def beside_last():
        for copy in early:
            copy.wait_recv()
        distance = lax.broadcasted_iota(jnp.int32, (128, 256), 1) - lax.broadcasted_iota(jnp.int32, (128, 256), 0)
        for other in range(2):
            rows = distance + 256 * (c if other == 0 else 1 - c)
            for k in range(4):
                for t in range(2):
                    first = jnp.broadcast_to(offsets[k, t][0:1, 0:1], (128, 256))
                    picks[other, k, t] = jnp.where(rows == first, 1.0, 0.0).astype(BF)

    def picked(other):
        half = c if other == 0 else 1 - c
        for k in range(4):
            slab = slabs[half, :, :, k].reshape(256, 128)
            for t in range(2):
                value = dot(picks[other, k, t], slab)
                if other == 0:
                    own_rows[k, t] = value
                else:
                    windows_out[t, 128 * k : 128 * k + 128, :] = (own_rows[k, t] + value).astype(BF)

    gathered(slabs, AG_I, CORE_GI, beside_last, picked)
    for i, copy in enumerate(steps):
        if i not in arrived:
            copy.wait_recv()
    for copy in sent + early + steps:
        copy.wait_send()


def back_kernel(windows, matrices, out_hbm, out, store_sem):
    stores = []
    for quarter in range(4):
        lines = pl.ds(8 * quarter, 8)
        for t in range(2):
            rows = pl.ds(256 * quarter, 256)
            side = jnp.concatenate([matrices[k, t, rows] for k in range(4)], axis=1)
            slope = (-STEP_LENGTH * dot(side, windows[t])).reshape(8, 32, 128)
            for part in range(2):
                out[part, lines, 32 * t : 32 * t + 32, :] = slope[:, :, 64 * part : 64 * part + 64]
        for part in range(2):
            store = pltpu.make_async_copy(
                out.at[part, lines], out_hbm.at[part, lines], store_sem.at[2 * quarter + part]
            )
            store.start()
            stores.append(store)
    for store in stores:
        store.wait()


def per_device(volume, tile_matrix, tile_offset, patch_count, scan_position, measured, illumination):
    any_space = pl.BlockSpec(memory_space=pl.ANY)
    vmem = pl.BlockSpec(memory_space=pltpu.VMEM)
    smem = pl.BlockSpec(memory_space=pltpu.SMEM)
    block = (4, 4, 2, 16, 256)
    tile_matrix = tile_matrix.reshape(2, 1024, 128)
    arrays = (volume, tile_matrix, measured.reshape(3, 256, 256), illumination, jnp.asarray(tables()))
    windows, matrices = pl.pallas_call(
        kernel,
        out_shape=(
            pltpu.VMEM((2, 512, 128), BF),
            pltpu.VMEM((4, 2, 1024, 128), BF),
        ),
        in_specs=[smem] * 3 + [any_space] * 5,
        out_specs=(vmem, vmem),
        scratch_shapes=[
            pltpu.VMEM((2, 32, 64, 256), BF),
            pltpu.VMEM((3, 256, 256), F32),
            pltpu.VMEM((2, 256, 256), F32),
            pltpu.VMEM((2, 512, 512), BF),
            pltpu.VMEM((4, 2, 8, 128), jnp.int32),
            pltpu.VMEM((2, 4, 896, 128), F32),
            pltpu.VMEM((3, 4, 768, 128), F32),
            pltpu.VMEM(block, BF),
            pltpu.VMEM(block, BF),
            pltpu.VMEM(block, F32),
            pltpu.VMEM(block, BF),
            pltpu.VMEM((15, 2, 16, 256), BF),
            pltpu.VMEM((2, 16, 256), F32),
            pltpu.VMEM((2, 16, 256), F32),
            pltpu.VMEM((2, *block), BF),
            pltpu.VMEM((2, 2, 512, 128), F32),
            pltpu.VMEM(block, BF),
            pltpu.VMEM(block, BF),
            pltpu.VMEM(block, F32),
            pltpu.VMEM(block, BF),
            pltpu.VMEM((15, 2, 16, 256), BF),
            pltpu.VMEM((4, 16, 128), F32),
            pltpu.VMEM((2, 4, 16, 128), F32),
            pltpu.VMEM((2, 4, 4, 4, 16, 128), BF),
            pltpu.VMEM((2, 4, 2, 128, 256), BF),
            pltpu.VMEM((4, 2, 128, 128), F32),
            pltpu.SemaphoreType.DMA((5,)),
            pltpu.SemaphoreType.DMA((N_SEMS,)),
            pltpu.SemaphoreType.DMA((N_SEMS,)),
        ],
        compiler_params=pltpu.CompilerParams(
            collective_id=0, has_side_effects=True, vmem_limit_bytes=44 * 2**20
        ),
    )(
        pltpu.with_memory_space_constraint(tile_offset, pltpu.HBM),
        patch_count,
        pltpu.with_memory_space_constraint(jnp.swapaxes(scan_position, 2, 3), pltpu.HBM),
        *(pltpu.with_memory_space_constraint(a, pltpu.HBM) for a in arrays),
    )
    return pl.pallas_call(
        back_kernel,
        out_shape=jax.ShapeDtypeStruct((2, 32, 64, 64), F32),
        in_specs=[vmem, vmem],
        out_specs=any_space,
        scratch_shapes=[
            pltpu.VMEM((2, 32, 64, 64), F32),
            pltpu.SemaphoreType.DMA((8,)),
        ],
        compiler_params=pltpu.CompilerParams(vmem_limit_bytes=44 * 2**20),
    )(*(pltpu.with_memory_space_constraint(a, pltpu.VMEM) for a in (windows, matrices)))


def solution(mesh):
    in_specs = (
        P(None, "vx", "vy", None),
        P("scan", "vx", "vy", None, None),
        P("scan", "vx", "vy"),
        P("scan", ("vx", "vy")),
        P("scan", ("vx", "vy"), None, None),
        P("scan", ("vx", "vy"), None, None, None),
        P(),
    )
    out_specs = P(None, "vx", "vy", "scan")
    return jax.shard_map(
        per_device, mesh=mesh, in_specs=in_specs, out_specs=out_specs, check_vma=False
    )
```
